512 devices in a mesh: leaf: 32 (over x_hi, z, core), tensor: 16 (over y, x_lo).
Axes of the slice: x: 4 (x_hi: 2, x_lo: 2; x = x_hi * 2 + x_lo), y: 8, z: 8, core: 2. Of those that a mesh axis runs over, the one named last changes fastest.
Arguments:
- trunk_kv: bfloat16 [32, 2048, 8, 256], P(None, ('leaf', 'tensor')), may hold values from -6 to 6
- slot_trees: int32 [32], replicated, may hold values from 0 to 31, each once
- trunk_len: int32 [32], replicated, may hold values from 256 to 2048, as said below
- parents: int32 [32, 384], P('leaf'), may hold values from -1 to 382, as said below
- queries: bfloat16 [32, 384, 8192], P('leaf', None, 'tensor'), may hold values from -12 to 12
- branch_kv: bfloat16 [32, 384, 8, 256], P('leaf', 'tensor'), may hold values from -9 to 9
Outputs:
- attended: bfloat16 [32, 384, 8192], P('leaf', None, 'tensor')
The draws below stay inside these ranges and needn't reach their ends.
Inputs may be any that keep to these rules, and one draw needn't show every extreme that they name: `slot_trees`: each tree is held by exactly one slot. `trunk_len`: every draw has a tree whose length is exactly 2048. parents[s, i] is -1 or one of the 4 tokens just before token i of the same slot; parents[s, 0] is -1.
All inputs are finite; a program needn't handle non-finite values.
Results may differ from the reference program's by a relative error of at most 0.0034.
Values may be sent and summed in bfloat16 or wider, within the bound.
A program may use at most 64 MiB of HBM per device.

```python
import math
import jax
import jax.numpy as jnp
from jax import lax

HQ = 64
KVH = 8
HD = 128
GROUP = 8
TRUNK = 2048
BR = 384
TREES = 32


def tree_parents(key):
    offsets = jax.random.randint(jax.random.fold_in(key, 101), (TREES, BR), 0, 4)
    places = jnp.arange(BR, dtype=jnp.int32)
    linked = jnp.maximum(places[None, :] - 1 - offsets, -1)
    return linked.at[0, BR - 1].set(BR - 2).astype(jnp.int32)


def draw_trunk_len(key, part):
    key = jax.random.fold_in(key, 7)
    length_key, pick_key = jax.random.split(key)
    lengths = jax.random.randint(length_key, (TREES,), TRUNK // 8, TRUNK + 1)
    longest = jax.random.randint(pick_key, (), 0, TREES)
    return jnp.where(jnp.arange(TREES, dtype=jnp.int32) == longest, TRUNK, lengths).astype(jnp.int32)


def draw_parents(key, part):
    linked = tree_parents(key)
    return linked


def draw_queries(key, part):
    key = jax.random.fold_in(key, 5)
    drawn = jnp.clip(2.0 * jax.random.normal(key, (TREES, BR, HQ * HD), jnp.float32), -12.0, 12.0)
    return drawn.astype(jnp.bfloat16)


def draw_branch_kv(key, part):
    key = jax.random.fold_in(key, 9)
    key_part, value_part = jax.random.split(key)
    full_shape = (TREES, BR, KVH, HD)
    key_rows = jnp.clip(1.5 * jax.random.normal(key_part, full_shape, jnp.float32), -9.0, 9.0)
    value_rows = jnp.clip(jax.random.normal(value_part, full_shape, jnp.float32), -6.0, 6.0)
    return jnp.concatenate([key_rows, value_rows], axis=-1).astype(jnp.bfloat16)


def block_levels(rng, dims, shards, low, top_value):
    def one(axis_at, blocks):
        draws = jax.random.uniform(jax.random.fold_in(jax.random.fold_in(rng, 6), axis_at), (blocks,), jnp.float32, low / len(shards), top_value / len(shards))
        return jnp.repeat(jnp.exp(draws), dims[axis_at] // blocks).reshape((-1,) + (1,) * (len(dims) - axis_at - 1))

    factor_of = one(*shards[0])
    for cut in shards[1:]:
        factor_of = factor_of * one(*cut)
    return factor_of


def normal_values(key, shape, scale, bound, cuts=(), kind=jnp.bfloat16):
    level = block_levels(key, shape, cuts, -0.22, 0.18) if cuts else 1.0
    entries = jax.random.normal(key, shape, jnp.float32) * scale * level
    return jnp.minimum(jnp.maximum(entries, -bound), bound).astype(kind)


def setup_inputs(seed: int = 0) -> dict:
    keys = jax.random.split(jax.random.key(seed), 7)
    trunk_kv = normal_values(keys[0], (TREES, TRUNK, KVH, 2 * HD), 1.0, 6.0, ((1, 512),))
    slot_trees = jax.random.permutation(keys[1], TREES).astype(jnp.int32)
    trunk_len = draw_trunk_len(jax.random.fold_in(keys[6], 71), 0)
    parents = draw_parents(jax.random.fold_in(keys[6], 71), 0)
    queries = draw_queries(jax.random.fold_in(keys[6], 71), 0)
    branch_kv = draw_branch_kv(jax.random.fold_in(keys[6], 71), 0)
    return {"trunk_kv": trunk_kv, "slot_trees": slot_trees, "trunk_len": trunk_len, "parents": parents, "queries": queries, "branch_kv": branch_kv}


def visible_matrix(parent_row):
    row_count = parent_row.shape[0]
    places = jnp.arange(row_count, dtype=jnp.int32)

    def extend(row_id, reached):
        parent_id = parent_row[row_id]
        inherited = jnp.where(parent_id >= 0, reached[jnp.maximum(parent_id, 0)], 0)
        fresh = jnp.maximum(inherited, (places == row_id).astype(jnp.int32))
        return reached.at[row_id].set(fresh)
    return lax.fori_loop(0, row_count, extend, jnp.zeros((row_count, row_count), jnp.int32))

def reference(trunk_kv, slot_trees, trunk_len, parents, queries, branch_kv):
    score_scale = 1.0 / math.sqrt(HD)
    trunk_places = jnp.arange(TRUNK, dtype=jnp.int32)

    def one_slot(slot_id):
        tree_id = slot_trees[slot_id]
        length = trunk_len[tree_id]
        trunk_tree = trunk_kv[tree_id]
        branch_tree = branch_kv[slot_id]
        visible = visible_matrix(parents[slot_id]) > 0
        grouped = queries[slot_id].reshape(BR, KVH, GROUP, HD)
        live_keys = trunk_places < length

        def one_head(head_id):
            query_rows = grouped[:, head_id].astype(jnp.float32)
            trunk_keys = trunk_tree[:, head_id, :HD].astype(jnp.float32)
            trunk_values = trunk_tree[:, head_id, HD:].astype(jnp.float32)
            branch_keys = branch_tree[:, head_id, :HD].astype(jnp.float32)
            branch_values = branch_tree[:, head_id, HD:].astype(jnp.float32)
            trunk_scores = jnp.einsum('rgd,nd->grn', query_rows, trunk_keys) * score_scale
            trunk_scores = jnp.where(live_keys[None, None, :], trunk_scores, -jnp.inf)
            branch_scores = jnp.einsum('rgd,nd->grn', query_rows, branch_keys) * score_scale
            branch_scores = jnp.where(visible[None], branch_scores, -jnp.inf)
            row_top = jnp.maximum(lax.optimization_barrier(jnp.max(trunk_scores, axis=-1)), lax.optimization_barrier(jnp.max(branch_scores, axis=-1)))
            trunk_weights = jnp.exp(trunk_scores - row_top[..., None])
            branch_weights = jnp.exp(branch_scores - row_top[..., None])
            denominator = lax.optimization_barrier(jnp.sum(trunk_weights, axis=-1)) + lax.optimization_barrier(jnp.sum(branch_weights, axis=-1))
            trunk_rounded = lax.optimization_barrier(trunk_weights.astype(jnp.bfloat16)).astype(jnp.float32)
            branch_rounded = lax.optimization_barrier(branch_weights.astype(jnp.bfloat16)).astype(jnp.float32)
            summed = jnp.einsum('grn,nd->grd', trunk_rounded, trunk_values)
            summed = summed + jnp.einsum('grn,nd->grd', branch_rounded, branch_values)
            return summed / denominator[..., None]
        per_head = lax.map(one_head, jnp.arange(KVH, dtype=jnp.int32))
        return per_head.transpose(2, 0, 1, 3).reshape(BR, HQ * HD).astype(jnp.bfloat16)
    return lax.map(one_slot, jnp.arange(TREES, dtype=jnp.int32))
```

```python
import math

import jax
import jax.numpy as jnp
import numpy as np
from jax import lax
from jax.experimental import pallas as pl
from jax.experimental.pallas import tpu as pltpu
from jax.sharding import PartitionSpec as P

MESH = pl.DeviceIdType.MESH

HQ = 64
KVH = 8
HD = 128
BR = 384
TREES = 32
HEADS = 4
NZ = 8
NY = 8
CHUNKS = 4
DEAD = -1e30
SCORE_SCALE = math.log2(math.e) / math.sqrt(HD)

def head_order():
    picks = np.zeros((128, 128), np.float32)
    for head in range(8):
        for target in range(4):
            for pos in range(4):
                picks[head * 16 + target * 4 + pos, target * 32 + pos * 8 + head] = 1
    return picks


def target_order():
    picks = np.zeros((256, 256), np.float32)
    for source in range(16):
        for target in range(4):
            for pos in range(4):
                picks[target * 64 + source * 4 + pos, source * 16 + target * 4 + pos] = 1
    return picks


def branch_out_order():
    picks = np.zeros((384, 384), np.float32)
    for head in range(8):
        for half in range(2):
            for token in range(24):
                picks[head * 48 + half * 24 + token, half * 192 + token * 8 + head] = 1
    return picks


def branch_in_order():
    picks = np.zeros((2, 96, 96), np.float32)
    for x_lo in range(2):
        for half in range(2):
            for source in range(2):
                for token in range(24):
                    other = (source + x_lo) % 2
                    picks[x_lo, half * 48 + source * 24 + token, other * 48 + half * 24 + token] = 1
    return picks


def kernel(
    slots, lengths, trunk, branch, queries, parents, pick_head, pick_target, pick_out, pick_in,
    out,
    staged, landed, sorted_rows, keys_values, branch_staged, branch_landed, branch_kv,
    turned, shown, top, total, summed,
    send_a, recv_a, send_b, recv_b, send_r, recv_r, send_p, recv_p,
):
    leaf = lax.axis_index("leaf")
    tensor = lax.axis_index("tensor")
    xh, z, c = leaf // 16, (leaf // 2) % 8, leaf % 2
    y, xl = tensor // 2, tensor % 2

    def place(xh, z, c, y, xl):
        return ((xh * 8 + z) * 2 + c, y * 2 + xl)

    barrier = pltpu.get_barrier_semaphore()

    def greet_plane(step, _):
        pl.semaphore_signal(
            barrier, inc=1, device_id=place(xh, (z + step // 8) % 8, c, (y + step % 8) % 8, xl),
            device_id_type=MESH,
        )
        return 0

    lax.fori_loop(1, NZ * NY, greet_plane, 0)

    def ring_place(step):
        return place((xh + step // 4) % 2, z, (c + (step // 2) % 2) % 2, y, (xl + step % 2) % 2)

    for step in range(1, 8):
        pl.semaphore_signal(barrier, inc=1, device_id=ring_place(step), device_id_type=MESH)

    def offset_of(group):
        return jnp.where(group % 2 == 0, (group // 2 + 1) % 4, 7 - group // 2)

    def stage(group):
        z_to = (z + offset_of(group)) % 8
        rows = jnp.concatenate(
            [trunk[slots[((q // 2) * 8 + z_to) * 2 + q % 2]] for q in range(4)], axis=0
        )
        ordered = jnp.dot(pick_head[...], rows, preferred_element_type=jnp.float32)
        ordered = ordered.astype(jnp.bfloat16)
        for head in range(8):
            staged[group, head] = ordered[head * 16 : head * 16 + 16]

    def send_plane(group):
        z_to = (z + offset_of(group)) % 8
        for dy in (4, 3, 5, 2, 6, 1, 7, 0):
            y_to = (y + dy) % 8

            def send():
                pltpu.make_async_remote_copy(
                    src_ref=staged.at[group, y_to],
                    dst_ref=landed.at[group * 8 + dy],
                    send_sem=send_a,
                    recv_sem=recv_a.at[group // 2],
                    device_id=place(xh, z_to, c, y_to, xl),
                    device_id_type=MESH,
                ).start()

            if dy == 0:
                pl.when(group != 6)(send)
            else:
                send()

    def stage_and_send(group, _):
        stage(group)
        send_plane(group)
        return 0

    pl.semaphore_wait(barrier, NZ * NY - 1 + 7)
    lax.fori_loop(0, 4, stage_and_send, 0)

    rows = jnp.concatenate([branch[:, :HD], branch[:, HD:]], axis=0)
    ordered = jnp.dot(pick_out[...], rows, preferred_element_type=jnp.float32).astype(jnp.bfloat16)
    for head in range(8):
        branch_staged[head] = ordered[head * 48 : head * 48 + 48]
    for dy in (4, 3, 5, 2, 6, 1, 7):
        y_to = (y + dy) % 8
        pltpu.make_async_remote_copy(
            src_ref=branch_staged.at[y_to],
            dst_ref=branch_landed.at[0, dy],
            send_sem=send_r,
            recv_sem=recv_r,
            device_id=place(xh, z, c, y_to, xl),
            device_id_type=MESH,
        ).start()
    branch_landed[0, 0] = branch_staged[y]

    lax.fori_loop(4, 8, stage_and_send, 0)
    landed[48] = staged[6, y]

    above = lax.broadcasted_iota(jnp.int32, (BR, BR), 0)
    along = lax.broadcasted_iota(jnp.int32, (BR, BR), 1)
    linked = jnp.logical_or(above == parents[...], above == along)
    shown[...] = jnp.where(linked, 1.0, 0.0).astype(jnp.bfloat16)

    def lengthen(_, carry):
        reached = shown[...]
        longer = jnp.dot(reached, reached, preferred_element_type=jnp.float32)
        shown[...] = jnp.where(longer > 0.5, 1.0, 0.0).astype(jnp.bfloat16)
        return carry

    lax.fori_loop(0, 9, lengthen, 0)

    for head in range(HEADS):
        turned[head] = jnp.transpose(queries[:, head * HD : head * HD + HD])

    def wait_bytes(ref, sem):
        pltpu.make_async_copy(ref, ref, sem).wait()

    def pass_on(chunk):
        if chunk < 3:
            wait_bytes(landed.at[chunk * 16 : chunk * 16 + 16], recv_a.at[chunk])
        else:
            wait_bytes(landed.at[49:64], recv_a.at[chunk])
        rows = landed[chunk * 16 : chunk * 16 + 16].reshape(256, 256)
        ordered = jnp.dot(pick_target[...], rows, preferred_element_type=jnp.float32)
        ordered = ordered.astype(jnp.bfloat16)
        for target in range(4):
            sorted_rows[chunk, target] = ordered[target * 64 : target * 64 + 64]
        for step in (5, 7, 4, 6, 1, 3, 2):
            target = ((xh + step // 4) % 2) * 2 + (c + (step // 2) % 2) % 2
            pltpu.make_async_remote_copy(
                src_ref=sorted_rows.at[chunk, target],
                dst_ref=keys_values.at[chunk, step],
                send_sem=send_b,
                recv_sem=recv_b.at[chunk],
                device_id=ring_place(step),
                device_id_type=MESH,
            ).start()
        keys_values[chunk, 0] = sorted_rows[chunk, xh * 2 + c]

    def attend(keys, values, mask, first):
        def one_head(head, _):
            scores = jnp.dot(keys, turned[head], preferred_element_type=jnp.float32)
            scores = scores * SCORE_SCALE + mask
            best = jnp.max(scores, axis=0, keepdims=True)
            if not first:
                best = jnp.maximum(best, top[head])
            weights = jnp.exp2(scores - best)
            weight_sum = jnp.sum(weights, axis=0, keepdims=True)
            product = lax.dot_general(
                values, weights.astype(jnp.bfloat16), (((0,), (0,)), ((), ())),
                preferred_element_type=jnp.float32,
            )
            if first:
                total[head] = weight_sum
                summed[head] = product
            else:
                fade = jnp.exp2(top[head] - best)
                total[head] = total[head] * fade + weight_sum
                summed[head] = summed[head] * fade + product
            top[head] = best
            return 0

        lax.fori_loop(0, HEADS, one_head, 0)

    length = lengths[slots[leaf]]

    def attend_chunk(chunk):
        wait_bytes(keys_values.at[chunk, 1:8], recv_b.at[chunk])
        both = keys_values[chunk].reshape(512, 256)
        key = lax.broadcasted_iota(jnp.int32, (512, 1), 0)
        source = key >> 6
        xh_from = (xh + (source >> 2)) & 1
        c_from = (c + ((source >> 1) & 1)) & 1
        xl_from = (xl + (source & 1)) & 1
        dz = jnp.where(((key >> 5) & 1) == 0, (chunk + 1) % 4, 7 - chunk)
        z_from = (z - dz + 8) & 7
        y_from = (y - ((key >> 2) & 7) + 8) & 7
        position = (((xh_from * 8 + z_from) * 2 + c_from) * 16 + y_from * 2 + xl_from) * 4 + (key & 3)
        mask = jnp.where(position < length, 0.0, DEAD)
        attend(both[:, :HD], both[:, HD:], mask, False)

    def attend_branch():
        wait_bytes(branch_landed.at[1], recv_p)
        order = pick_in[xl]
        for dy in range(8):
            y_from = (y - dy + 8) % 8
            rows = jnp.concatenate([branch_landed[0, dy], branch_landed[1, dy]], axis=0)
            ordered = jnp.dot(order, rows, preferred_element_type=jnp.float32).astype(jnp.bfloat16)
            branch_kv[0, y_from] = ordered[:48]
            branch_kv[1, y_from] = ordered[48:]
        mask = jnp.where(shown[...] > 0.5, 0.0, DEAD)
        attend(branch_kv[0].reshape(BR, HD), branch_kv[1].reshape(BR, HD), mask, True)

    pass_on(0)
    pass_on(1)
    wait_bytes(branch_landed.at[0, 1:8], recv_r)
    pltpu.make_async_remote_copy(
        src_ref=branch_landed.at[0],
        dst_ref=branch_landed.at[1],
        send_sem=send_p,
        recv_sem=recv_p,
        device_id=ring_place(1),
        device_id_type=MESH,
    ).start()
    pass_on(2)
    attend_branch()
    attend_chunk(0)
    pass_on(3)
    attend_chunk(1)
    attend_chunk(2)
    attend_chunk(3)

    for head in range(HEADS):
        result = summed[head] / total[head]
        out[:, head * HD : head * HD + HD] = jnp.transpose(result).astype(jnp.bfloat16)

    wait_bytes(landed.at[1:64], send_a)
    wait_bytes(branch_landed.at[0, 1:8], send_r)
    wait_bytes(branch_landed.at[0], send_p)
    wait_bytes(keys_values.at[:, 1:8], send_b)


def local(trunk_kv, slot_trees, trunk_len, parents, queries, branch_kv):
    vmem = pl.BlockSpec(memory_space=pltpu.VMEM)
    smem = pl.BlockSpec(memory_space=pltpu.SMEM)
    picks = [
        jnp.asarray(table(), dtype=jnp.bfloat16)
        for table in (head_order, target_order, branch_out_order, branch_in_order)
    ]
    attended = pl.pallas_call(
        kernel,
        out_shape=jax.ShapeDtypeStruct((BR, HEADS * HD), jnp.bfloat16),
        in_specs=[smem, smem] + [vmem] * 8,
        out_specs=vmem,
        scratch_shapes=[
            pltpu.VMEM((8, 8, 16, 256), jnp.bfloat16),
            pltpu.VMEM((64, 16, 256), jnp.bfloat16),
            pltpu.VMEM((CHUNKS, 4, 64, 256), jnp.bfloat16),
            pltpu.VMEM((CHUNKS, 8, 64, 256), jnp.bfloat16),
            pltpu.VMEM((8, 48, HD), jnp.bfloat16),
            pltpu.VMEM((2, 8, 48, HD), jnp.bfloat16),
            pltpu.VMEM((2, 8, 48, HD), jnp.bfloat16),
            pltpu.VMEM((HEADS, HD, BR), jnp.bfloat16),
            pltpu.VMEM((BR, BR), jnp.bfloat16),
            pltpu.VMEM((HEADS, 1, BR), jnp.float32),
            pltpu.VMEM((HEADS, 1, BR), jnp.float32),
            pltpu.VMEM((HEADS, HD, BR), jnp.float32),
            pltpu.SemaphoreType.DMA,
            pltpu.SemaphoreType.DMA((CHUNKS,)),
            pltpu.SemaphoreType.DMA,
            pltpu.SemaphoreType.DMA((CHUNKS,)),
            pltpu.SemaphoreType.DMA,
            pltpu.SemaphoreType.DMA,
            pltpu.SemaphoreType.DMA,
            pltpu.SemaphoreType.DMA,
        ],
        compiler_params=pltpu.CompilerParams(
            collective_id=0, has_side_effects=True, vmem_limit_bytes=40 * 1024 * 1024
        ),
    )(
        slot_trees,
        trunk_len,
        trunk_kv.reshape(TREES, 32, 2 * HD),
        branch_kv.reshape(192, 2 * HD),
        queries.reshape(BR, HEADS * HD),
        parents,
        *picks,
    )
    return attended.reshape(1, BR, HEADS * HD)


def solution(mesh):
    in_specs = (
        P(None, ("leaf", "tensor"), None, None),
        P(),
        P(),
        P("leaf", None),
        P("leaf", None, "tensor"),
        P("leaf", "tensor", None, None),
    )
    out_specs = P("leaf", None, "tensor")
    return jax.shard_map(local, mesh=mesh, in_specs=in_specs, out_specs=out_specs, check_vma=False)
```

```python
import math

import jax
import jax.numpy as jnp
from jax import lax
from jax.experimental import pallas as pl
from jax.experimental.pallas import tpu as pltpu
from jax.sharding import PartitionSpec as P

MESH = pl.DeviceIdType.MESH

HD = 128
BR = 384
TREES = 32
HEADS = 4
PAIRS = 2
WIDE = 2 * BR
NZ = 8
NY = 8
CHUNKS = 4
DEAD = -1e30
SCORE_SCALE = math.log2(math.e) / math.sqrt(HD)


def picks(target, rows, columns):
    row = lax.broadcasted_iota(jnp.int32, (rows, columns), 0)
    column = lax.broadcasted_iota(jnp.int32, (rows, columns), 1)
    return jnp.where(row == target(column), 1.0, 0.0).astype(jnp.bfloat16)


def moved(order, rows):
    return jnp.dot(order, rows, preferred_element_type=jnp.float32).astype(jnp.bfloat16)


def kernel(
    slots, lengths, trunk_hbm, branch_hbm, queries_hbm, parents_hbm,
    out,
    trunk, branch, queries, parents, pick_head, pick_target,
    staged, landed, sorted_rows, keys_values, branch_staged, branch_landed, branch_kv,
    turned, shown, top, total, summed,
    load, send_a, recv_a, send_b, recv_b, recv_c, send_f, recv_f, send_r, recv_r, send_p, recv_p,
):
    leaf = lax.axis_index("leaf")
    tensor = lax.axis_index("tensor")
    xh, z, c = leaf // 16, (leaf // 2) % 8, leaf % 2
    y, xl = tensor // 2, tensor % 2

    loads = [
        pltpu.make_async_copy(far, near, load.at[which])
        for which, (far, near) in enumerate(
            [(trunk_hbm, trunk), (branch_hbm, branch), (parents_hbm, parents), (queries_hbm, queries)]
        )
    ]
    for one in loads:
        one.start()

    def place(xh, z, c, y, xl):
        return ((xh * 8 + z) * 2 + c, y * 2 + xl)

    def near(a, d, b):
        return place((xh + a) % 2, z, (c + b) % 2, y, (xl + d) % 2)

    barrier = pltpu.get_barrier_semaphore()
    direct = ((1, 1, 0), (1, 1, 1), (0, 1, 0), (0, 1, 1), (0, 0, 1))

    def greet(step, _):
        pl.semaphore_signal(
            barrier, inc=1, device_id=place(xh, (z + step // 8) % 8, c, (y + step % 8) % 8, xl),
            device_id_type=MESH,
        )
        return 0

    lax.fori_loop(1, NZ * NY, greet, 0)
    for flips in direct:
        pl.semaphore_signal(barrier, inc=1, device_id=near(*flips), device_id_type=MESH)

    pick_head[...] = picks(
        lambda i: (i & 7) * 16 + (i >> 5) * 4 + ((i >> 3) & 3), 128, 128
    )
    pick_target[...] = picks(
        lambda i: ((i >> 2) & 3) * 64 + (i >> 4) * 4 + (i & 3), 256, 256
    )

    def z_offset(chunk, member):
        return (chunk + 1) % 4 if member == 0 else 7 - chunk

    def stage(chunk):
        for member in range(2):
            z_to = (z + z_offset(chunk, member)) % 8
            rows = jnp.concatenate(
                [trunk[slots[((q // 2) * 8 + z_to) * 2 + q % 2]] for q in range(4)], axis=0
            )
            ordered = moved(pick_head[...], rows)
            for head in range(8):
                staged[chunk * 2 + member, head] = ordered[head * 16 : head * 16 + 16]

    def send_plane(chunk):
        for dy in (4, 3, 5, 2, 6, 1, 7, 0):
            y_to = (y + dy) % 8
            for member in range(2):
                group = chunk * 2 + member
                z_to = (z + z_offset(chunk, member)) % 8

                def send():
                    pltpu.make_async_remote_copy(
                        src_ref=staged.at[group, y_to],
                        dst_ref=landed.at[group * 8 + dy],
                        send_sem=send_a,
                        recv_sem=recv_a.at[chunk],
                        device_id=place(xh, z_to, c, y_to, xl),
                        device_id_type=MESH,
                    ).start()

                if dy == 0 and member == 0:
                    pl.when(chunk != 3)(send)
                else:
                    send()

    def stage_and_send(chunk, _):
        stage(chunk)
        send_plane(chunk)
        return 0

    loads[0].wait()
    pl.semaphore_wait(barrier, NZ * NY - 1 + len(direct))
    lax.fori_loop(0, 2, stage_and_send, 0)

    loads[1].wait()

    def branch_target(i):
        half = jnp.where(i >= 192, 1, 0)
        inner = i - 192 * half
        return (inner & 7) * 48 + half * 24 + (inner >> 3)

    rows = jnp.concatenate([branch[:, :HD], branch[:, HD:]], axis=0)
    ordered = moved(picks(branch_target, 384, 384), rows)
    for head in range(8):
        branch_staged[head] = ordered[head * 48 : head * 48 + 48]
    for dy in (4, 3, 5, 2, 6, 1, 7):
        y_to = (y + dy) % 8
        pltpu.make_async_remote_copy(
            src_ref=branch_staged.at[y_to],
            dst_ref=branch_landed.at[0, dy],
            send_sem=send_r,
            recv_sem=recv_r,
            device_id=place(xh, z, c, y_to, xl),
            device_id_type=MESH,
        ).start()
    branch_landed[0, 0] = branch_staged[y]

    def wait_bytes(ref, sem):
        pltpu.make_async_copy(ref, ref, sem).wait()

    def pass_on(chunk):
        if chunk < 3:
            wait_bytes(landed.at[chunk * 16 : chunk * 16 + 16], recv_a.at[chunk])
        else:
            wait_bytes(landed.at[49:64], recv_a.at[chunk])
        rows = landed[chunk * 16 : chunk * 16 + 16].reshape(256, 256)
        ordered = moved(pick_target[...], rows)
        for target in range(4):
            sorted_rows[chunk, target] = ordered[target * 64 : target * 64 + 64]
        for a, d, b in direct:
            target = ((xh + a) % 2) * 2 + (c + b) % 2
            pltpu.make_async_remote_copy(
                src_ref=sorted_rows.at[chunk, target],
                dst_ref=keys_values.at[chunk, a * 4 + d * 2 + b],
                send_sem=send_b,
                recv_sem=recv_c.at[chunk] if a else recv_b.at[chunk],
                device_id=near(a, d, b),
                device_id_type=MESH,
            ).start()
        keys_values[chunk, 0] = sorted_rows[chunk, xh * 2 + c]

    def hand_on(chunk):
        wait_bytes(keys_values.at[chunk, 6:8], recv_c.at[chunk])
        pltpu.make_async_remote_copy(
            src_ref=keys_values.at[chunk, 6:8],
            dst_ref=keys_values.at[chunk, 4:6],
            send_sem=send_f,
            recv_sem=recv_f.at[chunk],
            device_id=near(0, 1, 0),
            device_id_type=MESH,
        ).start()

    def attend(keys, values, mask, first):
        keys = jnp.concatenate([keys, keys], axis=1)
        values = jnp.transpose(values)
        mask = jnp.concatenate([mask] * (WIDE // mask.shape[1]), axis=1)
        for pair in range(PAIRS):
            scores = jnp.dot(keys, turned[pair], preferred_element_type=jnp.float32) + mask
            best = jnp.max(scores, axis=0, keepdims=True)
            if not first:
                best = jnp.maximum(best, top[pair])
            weights = jnp.exp2(scores - best)
            weight_sum = jnp.sum(weights, axis=0, keepdims=True)
            product = jnp.dot(
                values, weights.astype(jnp.bfloat16), preferred_element_type=jnp.float32
            )
            if first:
                total[pair] = weight_sum
                summed[pair] = product
            else:
                fade = jnp.exp2(top[pair] - best)
                total[pair] = total[pair] * fade + weight_sum
                summed[pair] = summed[pair] * fade + product
            top[pair] = best

    def attend_chunk(chunk):
        wait_bytes(keys_values.at[chunk, 1:4], recv_b.at[chunk])
        wait_bytes(keys_values.at[chunk, 4:6], recv_f.at[chunk])
        both = keys_values[chunk].reshape(512, 256)
        key = lax.broadcasted_iota(jnp.int32, (512, HD), 0)
        xh_from = (xh + (key >> 8)) & 1
        xl_from = (xl + (key >> 7)) & 1
        c_from = (c + (key >> 6)) & 1
        dz = jnp.where(((key >> 5) & 1) == 0, (chunk + 1) % 4, 7 - chunk)
        z_from = (z - dz + 8) & 7
        y_from = (y - ((key >> 2) & 7) + 8) & 7
        position = (((xh_from * 8 + z_from) * 2 + c_from) * 16 + y_from * 2 + xl_from) * 4 + (key & 3)
        mask = jnp.where(position < lengths[slots[leaf]], 0.0, DEAD)
        attend(both[:, :HD], both[:, HD:], mask, False)

    def attend_branch():
        wait_bytes(branch_landed.at[1], recv_p)

        def target(i):
            other = jnp.where(i >= 48, 1, 0)
            inner = i - 48 * other
            half = jnp.where(inner >= 24, 1, 0)
            return half * 48 + ((other + xl) & 1) * 24 + inner - 24 * half

        order = picks(target, 96, 96)
        for dy in range(8):
            y_from = (y - dy + 8) % 8
            rows = jnp.concatenate([branch_landed[0, dy], branch_landed[1, dy]], axis=0)
            ordered = moved(order, rows)
            branch_kv[0, y_from] = ordered[:48]
            branch_kv[1, y_from] = ordered[48:]
        attend(branch_kv[0].reshape(BR, HD), branch_kv[1].reshape(BR, HD), shown[...], True)

    def turn_queries():
        loads[3].wait()
        for head in range(HEADS):
            flipped = jnp.transpose(queries[:, head * HD : head * HD + HD])
            scaled = flipped.astype(jnp.float32) * SCORE_SCALE
            coarse = scaled.astype(jnp.bfloat16)
            fine = (scaled - coarse.astype(jnp.float32)).astype(jnp.bfloat16)
            columns = slice((head % 2) * BR, (head % 2) * BR + BR)
            turned[head // 2, :HD, columns] = coarse
            turned[head // 2, HD:, columns] = fine

    def mark_ancestors():
        loads[2].wait()
        above = lax.broadcasted_iota(jnp.int32, (HD, HD), 0)
        along = lax.broadcasted_iota(jnp.int32, (HD, HD), 1)

        def links(up, down):
            return above + up * HD == parents[:, down * HD : down * HD + HD]

        def as_picks(wanted):
            return jnp.where(wanted, 1.0, 0.0).astype(jnp.bfloat16)

        within = [as_picks(jnp.logical_or(links(b, b), above == along)) for b in range(3)]
        for _ in range(7):
            within = [
                as_picks(jnp.dot(one, one, preferred_element_type=jnp.float32) > 0.5)
                for one in within
            ]
        step_one = moved(as_picks(links(0, 1)), within[1])
        step_two = moved(as_picks(links(1, 2)), within[2])
        zero_one = moved(within[0], step_one)
        blocks = {
            (0, 0): within[0], (1, 1): within[1], (2, 2): within[2],
            (0, 1): zero_one, (1, 2): moved(within[1], step_two), (0, 2): moved(zero_one, step_two),
        }
        for up in range(3):
            for down in range(3):
                if (up, down) in blocks:
                    mask = jnp.where(blocks[up, down].astype(jnp.float32) > 0.5, 0.0, DEAD)
                else:
                    mask = jnp.full((HD, HD), DEAD, jnp.float32)
                shown[up * HD : up * HD + HD, down * HD : down * HD + HD] = mask

    lax.fori_loop(2, 3, stage_and_send, 0)
    pass_on(0)
    lax.fori_loop(3, 4, stage_and_send, 0)
    landed[48] = staged[6, y]
    pass_on(1)
    hand_on(0)
    turn_queries()
    wait_bytes(branch_landed.at[0, 1:8], recv_r)
    pltpu.make_async_remote_copy(
        src_ref=branch_landed.at[0],
        dst_ref=branch_landed.at[1],
        send_sem=send_p,
        recv_sem=recv_p,
        device_id=near(0, 1, 0),
        device_id_type=MESH,
    ).start()
    mark_ancestors()
    pass_on(2)
    hand_on(1)
    attend_branch()
    pass_on(3)
    hand_on(2)
    attend_chunk(0)
    hand_on(3)
    attend_chunk(1)
    attend_chunk(2)
    attend_chunk(3)

    for head in range(HEADS):
        columns = slice((head % 2) * BR, (head % 2) * BR + BR)
        result = summed[head // 2, :, columns] * (1.0 / total[head // 2, :, columns])
        out[:, head * HD : head * HD + HD] = jnp.transpose(result.astype(jnp.bfloat16))

    wait_bytes(landed.at[1:64], send_a)
    wait_bytes(branch_landed.at[0, 1:8], send_r)
    wait_bytes(branch_landed.at[0], send_p)
    wait_bytes(keys_values.at[:, 0:5], send_b)
    wait_bytes(keys_values.at[:, 0:2], send_f)


def local(trunk_kv, slot_trees, trunk_len, parents, queries, branch_kv):
    smem = pl.BlockSpec(memory_space=pltpu.SMEM)
    hbm = pl.BlockSpec(memory_space=pltpu.HBM)
    bf16, f32 = jnp.bfloat16, jnp.float32
    attended = pl.pallas_call(
        kernel,
        out_shape=jax.ShapeDtypeStruct((BR, HEADS * HD), bf16),
        in_specs=[smem, smem, hbm, hbm, hbm, hbm],
        out_specs=pl.BlockSpec(memory_space=pltpu.VMEM),
        scratch_shapes=[
            pltpu.VMEM((TREES, 32, 256), bf16),
            pltpu.VMEM((192, 256), bf16),
            pltpu.VMEM((BR, HEADS * HD), bf16),
            pltpu.VMEM((1, BR), jnp.int32),
            pltpu.VMEM((128, 128), bf16),
            pltpu.VMEM((256, 256), bf16),
            pltpu.VMEM((8, 8, 16, 256), bf16),
            pltpu.VMEM((64, 16, 256), bf16),
            pltpu.VMEM((CHUNKS, 4, 64, 256), bf16),
            pltpu.VMEM((CHUNKS, 8, 64, 256), bf16),
            pltpu.VMEM((8, 48, HD), bf16),
            pltpu.VMEM((2, 8, 48, HD), bf16),
            pltpu.VMEM((2, 8, 48, HD), bf16),
            pltpu.VMEM((PAIRS, 2 * HD, WIDE), bf16),
            pltpu.VMEM((BR, BR), f32),
            pltpu.VMEM((PAIRS, 1, WIDE), f32),
            pltpu.VMEM((PAIRS, 1, WIDE), f32),
            pltpu.VMEM((PAIRS, HD, WIDE), f32),
            pltpu.SemaphoreType.DMA((4,)),
            pltpu.SemaphoreType.DMA,
            pltpu.SemaphoreType.DMA((CHUNKS,)),
            pltpu.SemaphoreType.DMA,
            pltpu.SemaphoreType.DMA((CHUNKS,)),
            pltpu.SemaphoreType.DMA((CHUNKS,)),
            pltpu.SemaphoreType.DMA,
            pltpu.SemaphoreType.DMA((CHUNKS,)),
            pltpu.SemaphoreType.DMA,
            pltpu.SemaphoreType.DMA,
            pltpu.SemaphoreType.DMA,
            pltpu.SemaphoreType.DMA,
        ],
        compiler_params=pltpu.CompilerParams(
            collective_id=0, has_side_effects=True, vmem_limit_bytes=60 * 1024 * 1024
        ),
    )(
        slot_trees,
        trunk_len,
        trunk_kv.reshape(TREES, 32, 2 * HD),
        branch_kv.reshape(192, 2 * HD),
        queries.reshape(BR, HEADS * HD),
        parents,
    )
    return attended.reshape(1, BR, HEADS * HD)


def solution(mesh):
    in_specs = (
        P(None, ("leaf", "tensor"), None, None),
        P(),
        P(),
        P("leaf", None),
        P("leaf", None, "tensor"),
        P("leaf", "tensor", None, None),
    )
    out_specs = P("leaf", None, "tensor")
    return jax.shard_map(local, mesh=mesh, in_specs=in_specs, out_specs=out_specs, check_vma=False)
```

```python
import math

import jax
import jax.numpy as jnp
from jax import lax
from jax.experimental import pallas as pl
from jax.experimental.pallas import tpu as pltpu
from jax.sharding import PartitionSpec as P

MESH = pl.DeviceIdType.MESH

HD = 128
BR = 384
TREES = 32
HEADS = 4
PAIRS = 2
WIDE = 2 * BR
CHUNKS = 4
OFFSETS = ((4, 7), (3, 5), (2, 6), (1, 0))
DEAD = -1e30
SCORE_SCALE = math.log2(math.e) / math.sqrt(HD)


def picks(target, rows, columns):
    row = lax.broadcasted_iota(jnp.int32, (rows, columns), 0)
    column = lax.broadcasted_iota(jnp.int32, (rows, columns), 1)
    return jnp.where(row == target(column), 1.0, 0.0).astype(jnp.bfloat16)


def moved(order, rows):
    return jnp.dot(order, rows, preferred_element_type=jnp.float32).astype(jnp.bfloat16)


def kernel(
    slots, lengths, trunk_hbm, branch_hbm, queries_hbm, parents_hbm,
    out,
    trunk, branch, queries, parents, pick_head, pick_target,
    staged, row_landed, plane_landed, sorted_rows, keys_values, branch_staged, branch_landed, branch_kv,
    turned, shown, top, total, summed, result,
    load, send_y, recv_y, send_z, recv_z, send_b, recv_b, recv_c, send_f, recv_f, send_r, recv_r, send_p, recv_p, store,
):
    leaf = lax.axis_index("leaf")
    tensor = lax.axis_index("tensor")
    xh, z, c = leaf // 16, (leaf // 2) % 8, leaf % 2
    y, xl = tensor // 2, tensor % 2

    loads = [
        pltpu.make_async_copy(there, here, load.at[which])
        for which, (there, here) in enumerate(
            [(trunk_hbm, trunk), (branch_hbm, branch), (parents_hbm, parents), (queries_hbm, queries)]
        )
    ]
    for one in loads:
        one.start()

    def place(xh, z, c, y, xl):
        return ((xh * 8 + z) * 2 + c, y * 2 + xl)

    def near(a, d, b):
        return place((xh + a) % 2, z, (c + b) % 2, y, (xl + d) % 2)

    barrier = pltpu.get_barrier_semaphore()
    direct = ((1, 1, 0), (1, 1, 1), (0, 1, 0), (0, 1, 1), (0, 0, 1))

    def signal(where):
        pl.semaphore_signal(barrier, inc=1, device_id=where, device_id_type=MESH)

    for step in range(1, 8):
        signal(place(xh, z, c, (y + step) % 8, xl))
        signal(place(xh, (z + step) % 8, c, y, xl))
    for flips in direct:
        signal(near(*flips))

    pick_head[...] = picks(
        lambda i: (i & 7) * 16 + (i >> 5) * 4 + ((i >> 3) & 3), 128, 128
    )
    pick_target[...] = picks(
        lambda i: ((i >> 2) & 3) * 64 + (i >> 4) * 4 + (i & 3), 256, 256
    )

    def send_row(chunk):
        for member, dz in enumerate(OFFSETS[chunk]):
            z_to = (z + dz) % 8
            rows = jnp.concatenate(
                [trunk[slots[((q // 2) * 8 + z_to) * 2 + q % 2]] for q in range(4)], axis=0
            )
            ordered = moved(pick_head[...], rows)
            for head in range(8):
                staged[chunk, head, member] = ordered[head * 16 : head * 16 + 16]
        for dy in (4, 3, 5, 2, 6, 1, 7):
            y_to = (y + dy) % 8
            pltpu.make_async_remote_copy(
                src_ref=staged.at[chunk, y_to],
                dst_ref=row_landed.at[chunk, :, dy],
                send_sem=send_y,
                recv_sem=recv_y.at[chunk],
                device_id=place(xh, z, c, y_to, xl),
                device_id_type=MESH,
            ).start()
        for member in range(2):
            row_landed[chunk, member, 0] = staged[chunk, y, member]

    loads[0].wait()
    pl.semaphore_wait(barrier, 14 + len(direct))
    send_row(0)
    send_row(1)

    loads[1].wait()

    def branch_target(i):
        half = jnp.where(i >= 192, 1, 0)
        inner = i - 192 * half
        return (inner & 7) * 48 + half * 24 + (inner >> 3)

    rows = jnp.concatenate([branch[:, :HD], branch[:, HD:]], axis=0)
    ordered = moved(picks(branch_target, 384, 384), rows)
    for head in range(8):
        branch_staged[head] = ordered[head * 48 : head * 48 + 48]
    for dy in (4, 3, 5, 2, 6, 1, 7):
        y_to = (y + dy) % 8
        pltpu.make_async_remote_copy(
            src_ref=branch_staged.at[y_to],
            dst_ref=branch_landed.at[0, dy],
            send_sem=send_r,
            recv_sem=recv_r,
            device_id=place(xh, z, c, y_to, xl),
            device_id_type=MESH,
        ).start()
    branch_landed[0, 0] = branch_staged[y]

    def wait_bytes(ref, sem):
        pltpu.make_async_copy(ref, ref, sem).wait()

    def send_plane(chunk):
        wait_bytes(row_landed.at[chunk, :, 1:8], recv_y.at[chunk])
        for member, dz in enumerate(OFFSETS[chunk]):
            if dz:
                pltpu.make_async_remote_copy(
                    src_ref=row_landed.at[chunk, member],
                    dst_ref=plane_landed.at[chunk * 2 + member],
                    send_sem=send_z,
                    recv_sem=recv_z.at[chunk],
                    device_id=place(xh, (z + dz) % 8, c, y, xl),
                    device_id_type=MESH,
                ).start()

    def pass_on(chunk):
        if chunk < 3:
            wait_bytes(plane_landed.at[chunk * 2 : chunk * 2 + 2], recv_z.at[chunk])
            rows = plane_landed[chunk * 2 : chunk * 2 + 2].reshape(256, 256)
        else:
            wait_bytes(plane_landed.at[6], recv_z.at[chunk])
            rows = jnp.concatenate(
                [plane_landed[6].reshape(128, 256), row_landed[3, 1].reshape(128, 256)], axis=0
            )
        ordered = moved(pick_target[...], rows)
        for target in range(4):
            sorted_rows[chunk, target] = ordered[target * 64 : target * 64 + 64]
        for a, d, b in direct:
            target = ((xh + a) % 2) * 2 + (c + b) % 2
            pltpu.make_async_remote_copy(
                src_ref=sorted_rows.at[chunk, target],
                dst_ref=keys_values.at[chunk, a * 4 + d * 2 + b],
                send_sem=send_b,
                recv_sem=recv_c.at[chunk] if a else recv_b.at[chunk],
                device_id=near(a, d, b),
                device_id_type=MESH,
            ).start()
        keys_values[chunk, 0] = sorted_rows[chunk, xh * 2 + c]

    def hand_on(chunk):
        wait_bytes(keys_values.at[chunk, 6:8], recv_c.at[chunk])
        pltpu.make_async_remote_copy(
            src_ref=keys_values.at[chunk, 6:8],
            dst_ref=keys_values.at[chunk, 4:6],
            send_sem=send_f,
            recv_sem=recv_f.at[chunk],
            device_id=near(0, 1, 0),
            device_id_type=MESH,
        ).start()

    def attend(keys, values, mask, first):
        keys = jnp.concatenate([keys, keys], axis=1)
        values = jnp.transpose(values)
        mask = jnp.concatenate([mask] * (WIDE // mask.shape[1]), axis=1)
        for pair in range(PAIRS):
            scores = jnp.dot(keys, turned[pair], preferred_element_type=jnp.float32) + mask
            best = jnp.max(scores, axis=0, keepdims=True)
            if not first:
                best = jnp.maximum(best, top[pair])
            weights = jnp.exp2(scores - best)
            weight_sum = jnp.sum(weights, axis=0, keepdims=True)
            product = jnp.dot(
                values, weights.astype(jnp.bfloat16), preferred_element_type=jnp.float32
            )
            if first:
                total[pair] = weight_sum
                summed[pair] = product
            else:
                fade = jnp.exp2(top[pair] - best)
                total[pair] = total[pair] * fade + weight_sum
                summed[pair] = summed[pair] * fade + product
            top[pair] = best

    def attend_chunk(chunk):
        wait_bytes(keys_values.at[chunk, 1:4], recv_b.at[chunk])
        wait_bytes(keys_values.at[chunk, 4:6], recv_f.at[chunk])
        both = keys_values[chunk].reshape(512, 256)
        key = lax.broadcasted_iota(jnp.int32, (512, HD), 0)
        xh_from = (xh + (key >> 8)) & 1
        xl_from = (xl + (key >> 7)) & 1
        c_from = (c + (key >> 6)) & 1
        dz = jnp.where(((key >> 5) & 1) == 0, OFFSETS[chunk][0], OFFSETS[chunk][1])
        z_from = (z - dz + 8) & 7
        y_from = (y - ((key >> 2) & 7) + 8) & 7
        position = (((xh_from * 8 + z_from) * 2 + c_from) * 16 + y_from * 2 + xl_from) * 4 + (key & 3)
        mask = jnp.where(position < lengths[slots[leaf]], 0.0, DEAD)
        attend(both[:, :HD], both[:, HD:], mask, False)

    def attend_branch():
        wait_bytes(branch_landed.at[1], recv_p)

        def target(i):
            other = jnp.where(i >= 48, 1, 0)
            inner = i - 48 * other
            half = jnp.where(inner >= 24, 1, 0)
            return half * 48 + ((other + xl) & 1) * 24 + inner - 24 * half

        order = picks(target, 96, 96)
        for dy in range(8):
            y_from = (y - dy + 8) % 8
            rows = jnp.concatenate([branch_landed[0, dy], branch_landed[1, dy]], axis=0)
            ordered = moved(order, rows)
            branch_kv[0, y_from] = ordered[:48]
            branch_kv[1, y_from] = ordered[48:]
        attend(branch_kv[0].reshape(BR, HD), branch_kv[1].reshape(BR, HD), shown[...], True)

    def turn_queries():
        loads[3].wait()
        for head in range(HEADS):
            flipped = jnp.transpose(queries[:, head * HD : head * HD + HD])
            scaled = flipped.astype(jnp.float32) * SCORE_SCALE
            coarse = scaled.astype(jnp.bfloat16)
            fine = (scaled - coarse.astype(jnp.float32)).astype(jnp.bfloat16)
            columns = slice((head % 2) * BR, (head % 2) * BR + BR)
            turned[head // 2, :HD, columns] = coarse
            turned[head // 2, HD:, columns] = fine

    def mark_ancestors():
        loads[2].wait()
        above = lax.broadcasted_iota(jnp.int32, (HD, HD), 0)
        along = lax.broadcasted_iota(jnp.int32, (HD, HD), 1)

        def links(up, down):
            return above + up * HD == parents[:, down * HD : down * HD + HD]

        def as_picks(wanted):
            return jnp.where(wanted, 1.0, 0.0).astype(jnp.bfloat16)

        within = [as_picks(jnp.logical_or(links(b, b), above == along)) for b in range(3)]
        for _ in range(7):
            within = [
                as_picks(jnp.dot(one, one, preferred_element_type=jnp.float32) > 0.5)
                for one in within
            ]
        step_one = moved(as_picks(links(0, 1)), within[1])
        step_two = moved(as_picks(links(1, 2)), within[2])
        zero_one = moved(within[0], step_one)
        blocks = {
            (0, 0): within[0], (1, 1): within[1], (2, 2): within[2],
            (0, 1): zero_one, (1, 2): moved(within[1], step_two), (0, 2): moved(zero_one, step_two),
        }
        for up in range(3):
            for down in range(3):
                if (up, down) in blocks:
                    mask = jnp.where(blocks[up, down].astype(jnp.float32) > 0.5, 0.0, DEAD)
                else:
                    mask = jnp.full((HD, HD), DEAD, jnp.float32)
                shown[up * HD : up * HD + HD, down * HD : down * HD + HD] = mask

    send_plane(0)
    send_row(2)
    send_row(3)
    send_plane(1)
    turn_queries()
    pass_on(0)
    wait_bytes(branch_landed.at[0, 1:8], recv_r)
    pltpu.make_async_remote_copy(
        src_ref=branch_landed.at[0],
        dst_ref=branch_landed.at[1],
        send_sem=send_p,
        recv_sem=recv_p,
        device_id=near(0, 1, 0),
        device_id_type=MESH,
    ).start()
    mark_ancestors()
    pass_on(1)
    hand_on(0)
    send_plane(2)
    attend_branch()
    hand_on(1)
    pass_on(2)
    send_plane(3)
    attend_chunk(0)
    pass_on(3)
    hand_on(2)
    attend_chunk(1)
    hand_on(3)
    attend_chunk(2)
    attend_chunk(3)

    stores = []
    for head in range(HEADS):
        columns = slice((head % 2) * BR, (head % 2) * BR + BR)
        lanes = slice(head * HD, head * HD + HD)
        normal = summed[head // 2, :, columns] * (1.0 / total[head // 2, :, columns])
        result[:, lanes] = jnp.transpose(normal.astype(jnp.bfloat16))
        stores.append(pltpu.make_async_copy(result.at[:, lanes], out.at[:, lanes], store.at[head]))
        stores[-1].start()
    for one in stores:
        one.wait()

    wait_bytes(row_landed.at[:, :, 1:8], send_y)
    wait_bytes(plane_landed.at[0:7], send_z)
    wait_bytes(branch_landed.at[0, 1:8], send_r)
    wait_bytes(branch_landed.at[0], send_p)
    wait_bytes(keys_values.at[:, 0:5], send_b)
    wait_bytes(keys_values.at[:, 0:2], send_f)


def local(trunk_kv, slot_trees, trunk_len, parents, queries, branch_kv):
    smem = pl.BlockSpec(memory_space=pltpu.SMEM)
    hbm = pl.BlockSpec(memory_space=pltpu.HBM)
    bf16, f32 = jnp.bfloat16, jnp.float32
    attended = pl.pallas_call(
        kernel,
        out_shape=jax.ShapeDtypeStruct((BR, HEADS * HD), bf16),
        in_specs=[smem, smem, hbm, hbm, hbm, hbm],
        out_specs=hbm,
        scratch_shapes=[
            pltpu.VMEM((TREES, 32, 256), bf16),
            pltpu.VMEM((192, 256), bf16),
            pltpu.VMEM((BR, HEADS * HD), bf16),
            pltpu.VMEM((1, BR), jnp.int32),
            pltpu.VMEM((128, 128), bf16),
            pltpu.VMEM((256, 256), bf16),
            pltpu.VMEM((CHUNKS, 8, 2, 16, 256), bf16),
            pltpu.VMEM((CHUNKS, 2, 8, 16, 256), bf16),
            pltpu.VMEM((8, 8, 16, 256), bf16),
            pltpu.VMEM((CHUNKS, 4, 64, 256), bf16),
            pltpu.VMEM((CHUNKS, 8, 64, 256), bf16),
            pltpu.VMEM((8, 48, HD), bf16),
            pltpu.VMEM((2, 8, 48, HD), bf16),
            pltpu.VMEM((2, 8, 48, HD), bf16),
            pltpu.VMEM((PAIRS, 2 * HD, WIDE), bf16),
            pltpu.VMEM((BR, BR), f32),
            pltpu.VMEM((PAIRS, 1, WIDE), f32),
            pltpu.VMEM((PAIRS, 1, WIDE), f32),
            pltpu.VMEM((PAIRS, HD, WIDE), f32),
            pltpu.VMEM((BR, HEADS * HD), bf16),
            pltpu.SemaphoreType.DMA((4,)),
            pltpu.SemaphoreType.DMA,
            pltpu.SemaphoreType.DMA((CHUNKS,)),
            pltpu.SemaphoreType.DMA,
            pltpu.SemaphoreType.DMA((CHUNKS,)),
            pltpu.SemaphoreType.DMA,
            pltpu.SemaphoreType.DMA((CHUNKS,)),
            pltpu.SemaphoreType.DMA((CHUNKS,)),
            pltpu.SemaphoreType.DMA,
            pltpu.SemaphoreType.DMA((CHUNKS,)),
            pltpu.SemaphoreType.DMA,
            pltpu.SemaphoreType.DMA,
            pltpu.SemaphoreType.DMA,
            pltpu.SemaphoreType.DMA,
            pltpu.SemaphoreType.DMA((HEADS,)),
        ],
        compiler_params=pltpu.CompilerParams(
            collective_id=0, has_side_effects=True, vmem_limit_bytes=60 * 1024 * 1024
        ),
    )(
        slot_trees,
        trunk_len,
        trunk_kv.reshape(TREES, 32, 2 * HD),
        branch_kv.reshape(192, 2 * HD),
        queries.reshape(BR, HEADS * HD),
        parents,
    )
    return attended.reshape(1, BR, HEADS * HD)


def solution(mesh):
    in_specs = (
        P(None, ("leaf", "tensor"), None, None),
        P(),
        P(),
        P("leaf", None),
        P("leaf", None, "tensor"),
        P("leaf", "tensor", None, None),
    )
    out_specs = P("leaf", None, "tensor")
    return jax.shard_map(local, mesh=mesh, in_specs=in_specs, out_specs=out_specs, check_vma=False)
```

```python
import math

import jax
import jax.numpy as jnp
from jax import lax
from jax.experimental import pallas as pl
from jax.experimental.pallas import tpu as pltpu
from jax.sharding import PartitionSpec as P

MESH = pl.DeviceIdType.MESH

HD = 128
BR = 384
TREES = 32
HEADS = 4
PAIRS = 2
WIDE = 2 * BR
NZ = 8
NY = 8
CHUNKS = 4
DEAD = -1e30
SCORE_SCALE = math.log2(math.e) / math.sqrt(HD)


def picks(target, rows, columns):
    row = lax.broadcasted_iota(jnp.int32, (rows, columns), 0)
    column = lax.broadcasted_iota(jnp.int32, (rows, columns), 1)
    return jnp.where(row == target(column), 1.0, 0.0).astype(jnp.bfloat16)


def moved(order, rows):
    return jnp.dot(order, rows, preferred_element_type=jnp.float32).astype(jnp.bfloat16)


def kernel(
    slots, lengths, trunk_hbm, branch_hbm, queries_hbm, parents_hbm,
    out,
    trunk, branch, queries, parents, pick_head, pick_target,
    staged, landed, sorted_rows, keys_values, branch_staged, branch_landed, branch_kv,
    turned, shown, top, total, summed,
    load, send_a, recv_a, send_b, recv_b, recv_c, send_f, recv_f, send_r, recv_r, send_p, recv_p,
):
    leaf = lax.axis_index("leaf")
    tensor = lax.axis_index("tensor")
    xh, z, c = leaf // 16, (leaf // 2) % 8, leaf % 2
    y, xl = tensor // 2, tensor % 2

    loads = [
        pltpu.make_async_copy(far, near, load.at[which])
        for which, (far, near) in enumerate(
            [(trunk_hbm, trunk), (branch_hbm, branch), (parents_hbm, parents), (queries_hbm, queries)]
        )
    ]
    for one in loads:
        one.start()

    def place(xh, z, c, y, xl):
        return ((xh * 8 + z) * 2 + c, y * 2 + xl)

    def near(a, d, b):
        return place((xh + a) % 2, z, (c + b) % 2, y, (xl + d) % 2)

    barrier = pltpu.get_barrier_semaphore()
    direct = ((1, 1, 0), (1, 1, 1), (0, 1, 0), (0, 1, 1), (0, 0, 1))

    def greet(step, _):
        pl.semaphore_signal(
            barrier, inc=1, device_id=place(xh, (z + step // 8) % 8, c, (y + step % 8) % 8, xl),
            device_id_type=MESH,
        )
        return 0

    lax.fori_loop(1, NZ * NY, greet, 0)
    for flips in direct:
        pl.semaphore_signal(barrier, inc=1, device_id=near(*flips), device_id_type=MESH)

    pick_head[...] = picks(
        lambda i: (i & 7) * 16 + (i >> 5) * 4 + ((i >> 3) & 3), 128, 128
    )
    pick_target[...] = picks(
        lambda i: ((i >> 2) & 3) * 64 + (i >> 4) * 4 + (i & 3), 256, 256
    )

    def z_offset(chunk, member):
        return (chunk + 1) % 4 if member == 0 else 7 - chunk

    def stage(chunk):
        for member in range(2):
            z_to = (z + z_offset(chunk, member)) % 8
            rows = jnp.concatenate(
                [trunk[slots[((q // 2) * 8 + z_to) * 2 + q % 2]] for q in range(4)], axis=0
            )
            ordered = moved(pick_head[...], rows)
            for head in range(8):
                staged[chunk * 2 + member, head] = ordered[head * 16 : head * 16 + 16]

    def send_plane(chunk):
        for dy in (4, 3, 5, 2, 6, 1, 7, 0):
            y_to = (y + dy) % 8
            for member in range(2):
                group = chunk * 2 + member
                z_to = (z + z_offset(chunk, member)) % 8

                def send():
                    pltpu.make_async_remote_copy(
                        src_ref=staged.at[group, y_to],
                        dst_ref=landed.at[group * 8 + dy],
                        send_sem=send_a,
                        recv_sem=recv_a.at[chunk],
                        device_id=place(xh, z_to, c, y_to, xl),
                        device_id_type=MESH,
                    ).start()

                if dy == 0 and member == 0:
                    pl.when(chunk != 3)(send)
                else:
                    send()

    def stage_and_send(chunk, _):
        stage(chunk)
        send_plane(chunk)
        return 0

    loads[0].wait()
    pl.semaphore_wait(barrier, NZ * NY - 1 + len(direct))
    lax.fori_loop(0, 1, stage_and_send, 0)

    loads[1].wait()

    def branch_target(i):
        half = jnp.where(i >= 192, 1, 0)
        inner = i - 192 * half
        return (inner & 7) * 48 + half * 24 + (inner >> 3)

    rows = jnp.concatenate([branch[:, :HD], branch[:, HD:]], axis=0)
    ordered = moved(picks(branch_target, 384, 384), rows)
    for head in range(8):
        branch_staged[head] = ordered[head * 48 : head * 48 + 48]
    for dy in (4, 3, 5, 2, 6, 1, 7):
        y_to = (y + dy) % 8
        pltpu.make_async_remote_copy(
            src_ref=branch_staged.at[y_to],
            dst_ref=branch_landed.at[0, dy],
            send_sem=send_r,
            recv_sem=recv_r,
            device_id=place(xh, z, c, y_to, xl),
            device_id_type=MESH,
        ).start()
    branch_landed[0, 0] = branch_staged[y]

    def wait_bytes(ref, sem):
        pltpu.make_async_copy(ref, ref, sem).wait()

    def pass_on(chunk):
        if chunk < 3:
            wait_bytes(landed.at[chunk * 16 : chunk * 16 + 16], recv_a.at[chunk])
        else:
            wait_bytes(landed.at[49:64], recv_a.at[chunk])
        rows = landed[chunk * 16 : chunk * 16 + 16].reshape(256, 256)
        ordered = moved(pick_target[...], rows)
        for target in range(4):
            sorted_rows[chunk, target] = ordered[target * 64 : target * 64 + 64]
        for a, d, b in direct:
            target = ((xh + a) % 2) * 2 + (c + b) % 2
            pltpu.make_async_remote_copy(
                src_ref=sorted_rows.at[chunk, target],
                dst_ref=keys_values.at[chunk, a * 4 + d * 2 + b],
                send_sem=send_b,
                recv_sem=recv_c.at[chunk] if a else recv_b.at[chunk],
                device_id=near(a, d, b),
                device_id_type=MESH,
            ).start()
        keys_values[chunk, 0] = sorted_rows[chunk, xh * 2 + c]

    def hand_on(chunk):
        wait_bytes(keys_values.at[chunk, 6:8], recv_c.at[chunk])
        pltpu.make_async_remote_copy(
            src_ref=keys_values.at[chunk, 6:8],
            dst_ref=keys_values.at[chunk, 4:6],
            send_sem=send_f,
            recv_sem=recv_f.at[chunk],
            device_id=near(0, 1, 0),
            device_id_type=MESH,
        ).start()

    def attend(keys, values, mask, first):
        keys = jnp.concatenate([keys, keys], axis=1)
        values = jnp.transpose(values)
        mask = jnp.concatenate([mask] * (WIDE // mask.shape[1]), axis=1)
        for pair in range(PAIRS):
            scores = jnp.dot(keys, turned[pair], preferred_element_type=jnp.float32) + mask
            best = jnp.max(scores, axis=0, keepdims=True)
            if not first:
                best = jnp.maximum(best, top[pair])
            weights = jnp.exp2(scores - best)
            weight_sum = jnp.sum(weights, axis=0, keepdims=True)
            product = jnp.dot(
                values, weights.astype(jnp.bfloat16), preferred_element_type=jnp.float32
            )
            if first:
                total[pair] = weight_sum
                summed[pair] = product
            else:
                fade = jnp.exp2(top[pair] - best)
                total[pair] = total[pair] * fade + weight_sum
                summed[pair] = summed[pair] * fade + product
            top[pair] = best

    def attend_chunk(chunk):
        wait_bytes(keys_values.at[chunk, 1:4], recv_b.at[chunk])
        wait_bytes(keys_values.at[chunk, 4:6], recv_f.at[chunk])
        both = keys_values[chunk].reshape(512, 256)
        key = lax.broadcasted_iota(jnp.int32, (512, HD), 0)
        xh_from = (xh + (key >> 8)) & 1
        xl_from = (xl + (key >> 7)) & 1
        c_from = (c + (key >> 6)) & 1
        dz = jnp.where(((key >> 5) & 1) == 0, (chunk + 1) % 4, 7 - chunk)
        z_from = (z - dz + 8) & 7
        y_from = (y - ((key >> 2) & 7) + 8) & 7
        position = (((xh_from * 8 + z_from) * 2 + c_from) * 16 + y_from * 2 + xl_from) * 4 + (key & 3)
        mask = jnp.where(position < lengths[slots[leaf]], 0.0, DEAD)
        attend(both[:, :HD], both[:, HD:], mask, False)

    def attend_branch():
        wait_bytes(branch_landed.at[1], recv_p)

        def target(i):
            other = jnp.where(i >= 48, 1, 0)
            inner = i - 48 * other
            half = jnp.where(inner >= 24, 1, 0)
            return half * 48 + ((other + xl) & 1) * 24 + inner - 24 * half

        order = picks(target, 96, 96)
        for dy in range(8):
            y_from = (y - dy + 8) % 8
            rows = jnp.concatenate([branch_landed[0, dy], branch_landed[1, dy]], axis=0)
            ordered = moved(order, rows)
            branch_kv[0, y_from] = ordered[:48]
            branch_kv[1, y_from] = ordered[48:]
        attend(branch_kv[0].reshape(BR, HD), branch_kv[1].reshape(BR, HD), shown[...], True)

    def turn_queries():
        loads[3].wait()
        for head in range(HEADS):
            flipped = jnp.transpose(queries[:, head * HD : head * HD + HD])
            scaled = flipped.astype(jnp.float32) * SCORE_SCALE
            coarse = scaled.astype(jnp.bfloat16)
            fine = (scaled - coarse.astype(jnp.float32)).astype(jnp.bfloat16)
            columns = slice((head % 2) * BR, (head % 2) * BR + BR)
            turned[head // 2, :HD, columns] = coarse
            turned[head // 2, HD:, columns] = fine

    def mark_ancestors():
        loads[2].wait()
        above = lax.broadcasted_iota(jnp.int32, (HD, HD), 0)
        along = lax.broadcasted_iota(jnp.int32, (HD, HD), 1)

        def links(up, down):
            return above + up * HD == parents[:, down * HD : down * HD + HD]

        def as_picks(wanted):
            return jnp.where(wanted, 1.0, 0.0).astype(jnp.bfloat16)

        within = [as_picks(jnp.logical_or(links(b, b), above == along)) for b in range(3)]
        for _ in range(7):
            within = [
                as_picks(jnp.dot(one, one, preferred_element_type=jnp.float32) > 0.5)
                for one in within
            ]
        step_one = moved(as_picks(links(0, 1)), within[1])
        step_two = moved(as_picks(links(1, 2)), within[2])
        zero_one = moved(within[0], step_one)
        blocks = {
            (0, 0): within[0], (1, 1): within[1], (2, 2): within[2],
            (0, 1): zero_one, (1, 2): moved(within[1], step_two), (0, 2): moved(zero_one, step_two),
        }
        for up in range(3):
            for down in range(3):
                if (up, down) in blocks:
                    mask = jnp.where(blocks[up, down].astype(jnp.float32) > 0.5, 0.0, DEAD)
                else:
                    mask = jnp.full((HD, HD), DEAD, jnp.float32)
                shown[up * HD : up * HD + HD, down * HD : down * HD + HD] = mask

    def hand_branch():
        wait_bytes(branch_landed.at[0, 1:8], recv_r)
        pltpu.make_async_remote_copy(
            src_ref=branch_landed.at[0],
            dst_ref=branch_landed.at[1],
            send_sem=send_p,
            recv_sem=recv_p,
            device_id=near(0, 1, 0),
            device_id_type=MESH,
        ).start()

    lax.fori_loop(1, 2, stage_and_send, 0)
    turn_queries()
    pass_on(0)
    lax.fori_loop(2, 3, stage_and_send, 0)
    mark_ancestors()
    pass_on(1)
    lax.fori_loop(3, 4, stage_and_send, 0)
    landed[48] = staged[6, y]
    hand_on(0)
    hand_branch()
    pass_on(2)
    hand_on(1)
    attend_branch()
    pass_on(3)
    hand_on(2)
    attend_chunk(0)
    hand_on(3)
    attend_chunk(1)
    attend_chunk(2)
    attend_chunk(3)

    for head in range(HEADS):
        columns = slice((head % 2) * BR, (head % 2) * BR + BR)
        result = summed[head // 2, :, columns] * (1.0 / total[head // 2, :, columns])
        out[:, head * HD : head * HD + HD] = jnp.transpose(result.astype(jnp.bfloat16))

    wait_bytes(landed.at[1:64], send_a)
    wait_bytes(branch_landed.at[0, 1:8], send_r)
    wait_bytes(branch_landed.at[0], send_p)
    wait_bytes(keys_values.at[:, 0:5], send_b)
    wait_bytes(keys_values.at[:, 0:2], send_f)


def local(trunk_kv, slot_trees, trunk_len, parents, queries, branch_kv):
    smem = pl.BlockSpec(memory_space=pltpu.SMEM)
    hbm = pl.BlockSpec(memory_space=pltpu.HBM)
    bf16, f32 = jnp.bfloat16, jnp.float32
    attended = pl.pallas_call(
        kernel,
        out_shape=jax.ShapeDtypeStruct((BR, HEADS * HD), bf16),
        in_specs=[smem, smem, hbm, hbm, hbm, hbm],
        out_specs=pl.BlockSpec(memory_space=pltpu.VMEM),
        scratch_shapes=[
            pltpu.VMEM((TREES, 32, 256), bf16),
            pltpu.VMEM((192, 256), bf16),
            pltpu.VMEM((BR, HEADS * HD), bf16),
            pltpu.VMEM((1, BR), jnp.int32),
            pltpu.VMEM((128, 128), bf16),
            pltpu.VMEM((256, 256), bf16),
            pltpu.VMEM((8, 8, 16, 256), bf16),
            pltpu.VMEM((64, 16, 256), bf16),
            pltpu.VMEM((CHUNKS, 4, 64, 256), bf16),
            pltpu.VMEM((CHUNKS, 8, 64, 256), bf16),
            pltpu.VMEM((8, 48, HD), bf16),
            pltpu.VMEM((2, 8, 48, HD), bf16),
            pltpu.VMEM((2, 8, 48, HD), bf16),
            pltpu.VMEM((PAIRS, 2 * HD, WIDE), bf16),
            pltpu.VMEM((BR, BR), f32),
            pltpu.VMEM((PAIRS, 1, WIDE), f32),
            pltpu.VMEM((PAIRS, 1, WIDE), f32),
            pltpu.VMEM((PAIRS, HD, WIDE), f32),
            pltpu.SemaphoreType.DMA((4,)),
            pltpu.SemaphoreType.DMA,
            pltpu.SemaphoreType.DMA((CHUNKS,)),
            pltpu.SemaphoreType.DMA,
            pltpu.SemaphoreType.DMA((CHUNKS,)),
            pltpu.SemaphoreType.DMA((CHUNKS,)),
            pltpu.SemaphoreType.DMA,
            pltpu.SemaphoreType.DMA((CHUNKS,)),
            pltpu.SemaphoreType.DMA,
            pltpu.SemaphoreType.DMA,
            pltpu.SemaphoreType.DMA,
            pltpu.SemaphoreType.DMA,
        ],
        compiler_params=pltpu.CompilerParams(
            collective_id=0, has_side_effects=True, vmem_limit_bytes=60 * 1024 * 1024
        ),
    )(
        slot_trees,
        trunk_len,
        trunk_kv.reshape(TREES, 32, 2 * HD),
        branch_kv.reshape(192, 2 * HD),
        queries.reshape(BR, HEADS * HD),
        parents,
    )
    return attended.reshape(1, BR, HEADS * HD)


def solution(mesh):
    in_specs = (
        P(None, ("leaf", "tensor"), None, None),
        P(),
        P(),
        P("leaf", None),
        P("leaf", None, "tensor"),
        P("leaf", "tensor", None, None),
    )
    out_specs = P("leaf", None, "tensor")
    return jax.shard_map(local, mesh=mesh, in_specs=in_specs, out_specs=out_specs, check_vma=False)
```

```python
import math

import jax
import jax.numpy as jnp
from jax import lax
from jax.experimental import pallas as pl
from jax.experimental.pallas import tpu as pltpu
from jax.sharding import PartitionSpec as P

MESH = pl.DeviceIdType.MESH

HD = 128
BR = 384
TREES = 32
HEADS = 4
PAIRS = 2
WIDE = 2 * BR
NZ = 8
NY = 8
CHUNKS = 4
BLOCK = 64
DEAD = -1e30
SCORE_SCALE = math.log2(math.e) / math.sqrt(HD)


def picks(target, rows, columns):
    row = lax.broadcasted_iota(jnp.int32, (rows, columns), 0)
    column = lax.broadcasted_iota(jnp.int32, (rows, columns), 1)
    return jnp.where(row == target(column), 1.0, 0.0).astype(jnp.bfloat16)


def moved(order, rows):
    return jnp.dot(order, rows, preferred_element_type=jnp.float32).astype(jnp.bfloat16)


def kernel(
    slots, lengths, trunk_hbm, branch_hbm, queries_hbm, parents_hbm,
    out,
    trunk, branch, queries, parents, pick_head, pick_target,
    staged, landed, sorted_rows, keys_values, branch_staged, branch_landed, branch_kv,
    turned, shown, top, total, summed, dead, raw, rounded,
    load, send_a, recv_a, send_b, recv_b, recv_c, send_f, recv_f, send_r, recv_r, send_p, recv_p,
):
    leaf = lax.axis_index("leaf")
    tensor = lax.axis_index("tensor")
    xh, z, c = leaf // 16, (leaf // 2) % 8, leaf % 2
    y, xl = tensor // 2, tensor % 2

    loads = [
        pltpu.make_async_copy(far, near, load.at[which])
        for which, (far, near) in enumerate(
            [(trunk_hbm, trunk), (branch_hbm, branch), (parents_hbm, parents), (queries_hbm, queries)]
        )
    ]
    for one in loads:
        one.start()

    def place(xh, z, c, y, xl):
        return ((xh * 8 + z) * 2 + c, y * 2 + xl)

    def near(a, d, b):
        return place((xh + a) % 2, z, (c + b) % 2, y, (xl + d) % 2)

    barrier = pltpu.get_barrier_semaphore()
    direct = ((1, 1, 0), (1, 1, 1), (0, 1, 0), (0, 1, 1), (0, 0, 1))

    def greet(step, _):
        pl.semaphore_signal(
            barrier, inc=1, device_id=place(xh, (z + step // 8) % 8, c, (y + step % 8) % 8, xl),
            device_id_type=MESH,
        )
        return 0

    lax.fori_loop(1, NZ * NY, greet, 0)
    for flips in direct:
        pl.semaphore_signal(barrier, inc=1, device_id=near(*flips), device_id_type=MESH)

    pick_head[...] = picks(
        lambda i: (i & 7) * 16 + (i >> 5) * 4 + ((i >> 3) & 3), 128, 128
    )
    pick_target[...] = picks(
        lambda i: ((i >> 2) & 3) * 64 + (i >> 4) * 4 + (i & 3), 256, 256
    )

    def z_offset(chunk, member):
        return (chunk + 1) % 4 if member == 0 else 7 - chunk

    def stage(chunk):
        for member in range(2):
            z_to = (z + z_offset(chunk, member)) % 8
            rows = jnp.concatenate(
                [trunk[slots[((q // 2) * 8 + z_to) * 2 + q % 2]] for q in range(4)], axis=0
            )
            ordered = moved(pick_head[...], rows)
            for head in range(8):
                staged[chunk * 2 + member, head] = ordered[head * 16 : head * 16 + 16]

    def send_plane(chunk):
        for dy in (4, 3, 5, 2, 6, 1, 7, 0):
            y_to = (y + dy) % 8
            for member in range(2):
                group = chunk * 2 + member
                z_to = (z + z_offset(chunk, member)) % 8

                def send():
                    pltpu.make_async_remote_copy(
                        src_ref=staged.at[group, y_to],
                        dst_ref=landed.at[group * 8 + dy],
                        send_sem=send_a,
                        recv_sem=recv_a.at[chunk],
                        device_id=place(xh, z_to, c, y_to, xl),
                        device_id_type=MESH,
                    ).start()

                if dy == 0 and member == 0:
                    pl.when(chunk != 3)(send)
                else:
                    send()

    def stage_and_send(chunk, _):
        stage(chunk)
        send_plane(chunk)
        return 0

    loads[0].wait()
    pl.semaphore_wait(barrier, NZ * NY - 1 + len(direct))
    lax.fori_loop(0, 2, stage_and_send, 0)

    loads[1].wait()

    def branch_target(i):
        half = jnp.where(i >= 192, 1, 0)
        inner = i - 192 * half
        return (inner & 7) * 48 + half * 24 + (inner >> 3)

    rows = jnp.concatenate([branch[:, :HD], branch[:, HD:]], axis=0)
    ordered = moved(picks(branch_target, 384, 384), rows)
    for head in range(8):
        branch_staged[head] = ordered[head * 48 : head * 48 + 48]
    for dy in (4, 3, 5, 2, 6, 1, 7):
        y_to = (y + dy) % 8
        pltpu.make_async_remote_copy(
            src_ref=branch_staged.at[y_to],
            dst_ref=branch_landed.at[0, dy],
            send_sem=send_r,
            recv_sem=recv_r,
            device_id=place(xh, z, c, y_to, xl),
            device_id_type=MESH,
        ).start()
    branch_landed[0, 0] = branch_staged[y]

    def wait_bytes(ref, sem):
        pltpu.make_async_copy(ref, ref, sem).wait()

    def pass_on(chunk):
        if chunk < 3:
            wait_bytes(landed.at[chunk * 16 : chunk * 16 + 16], recv_a.at[chunk])
        else:
            wait_bytes(landed.at[49:64], recv_a.at[chunk])
        rows = landed[chunk * 16 : chunk * 16 + 16].reshape(256, 256)
        ordered = moved(pick_target[...], rows)
        for target in range(4):
            sorted_rows[chunk, target] = ordered[target * 64 : target * 64 + 64]
        for a, d, b in direct:
            target = ((xh + a) % 2) * 2 + (c + b) % 2
            pltpu.make_async_remote_copy(
                src_ref=sorted_rows.at[chunk, target],
                dst_ref=keys_values.at[chunk, a * 4 + d * 2 + b],
                send_sem=send_b,
                recv_sem=recv_c.at[chunk] if a else recv_b.at[chunk],
                device_id=near(a, d, b),
                device_id_type=MESH,
            ).start()
        keys_values[chunk, 0] = sorted_rows[chunk, xh * 2 + c]

    def hand_on(chunk):
        wait_bytes(keys_values.at[chunk, 6:8], recv_c.at[chunk])
        pltpu.make_async_remote_copy(
            src_ref=keys_values.at[chunk, 6:8],
            dst_ref=keys_values.at[chunk, 4:6],
            send_sem=send_f,
            recv_sem=recv_f.at[chunk],
            device_id=near(0, 1, 0),
            device_id_type=MESH,
        ).start()

    def attend(keys, values, mask_rows, first):
        count = keys.shape[0]
        keys = jnp.concatenate([keys, keys], axis=1)
        values = jnp.transpose(values)
        blocks = [slice(at, at + BLOCK) for at in range(0, count, BLOCK)]
        for pair in range(PAIRS):
            raw[pair, :count] = jnp.dot(keys, turned[pair], preferred_element_type=jnp.float32)
        for pair in range(PAIRS):
            fades = []
            for half in range(2):
                columns = slice(half * BR, half * BR + BR)
                best = None if first else top[pair, :, columns]
                for block in blocks:
                    scores = raw[pair, block, columns] + mask_rows(block)
                    highest = jnp.max(scores, axis=0, keepdims=True)
                    best = highest if best is None else jnp.maximum(best, highest)
                weight_sum = None
                for block in blocks:
                    weights = jnp.exp2(raw[pair, block, columns] + mask_rows(block) - best)
                    part = jnp.sum(weights, axis=0, keepdims=True)
                    weight_sum = part if weight_sum is None else weight_sum + part
                    rounded[pair, block, columns] = weights.astype(jnp.bfloat16)
                if not first:
                    fades.append(jnp.exp2(top[pair, :, columns] - best))
                    weight_sum = total[pair, :, columns] * fades[half] + weight_sum
                total[pair, :, columns] = weight_sum
                top[pair, :, columns] = best
            product = jnp.dot(
                values, rounded[pair, :count], preferred_element_type=jnp.float32
            )
            for half in range(2):
                columns = slice(half * BR, half * BR + BR)
                if first:
                    summed[pair, :, columns] = product[:, columns]
                else:
                    summed[pair, :, columns] = (
                        summed[pair, :, columns] * fades[half] + product[:, columns]
                    )

    def attend_chunk(chunk):
        wait_bytes(keys_values.at[chunk, 1:4], recv_b.at[chunk])
        wait_bytes(keys_values.at[chunk, 4:6], recv_f.at[chunk])
        both = keys_values[chunk].reshape(512, 256)
        key = lax.broadcasted_iota(jnp.int32, (512, HD), 0)
        xh_from = (xh + (key >> 8)) & 1
        xl_from = (xl + (key >> 7)) & 1
        c_from = (c + (key >> 6)) & 1
        dz = jnp.where(((key >> 5) & 1) == 0, (chunk + 1) % 4, 7 - chunk)
        z_from = (z - dz + 8) & 7
        y_from = (y - ((key >> 2) & 7) + 8) & 7
        position = (((xh_from * 8 + z_from) * 2 + c_from) * 16 + y_from * 2 + xl_from) * 4 + (key & 3)
        dead[...] = jnp.where(position < lengths[slots[leaf]], 0.0, DEAD)
        attend(
            both[:, :HD], both[:, HD:],
            lambda block: jnp.concatenate([dead[block]] * (BR // HD), axis=1), False,
        )

    def attend_branch():
        wait_bytes(branch_landed.at[1], recv_p)

        def target(i):
            other = jnp.where(i >= 48, 1, 0)
            inner = i - 48 * other
            half = jnp.where(inner >= 24, 1, 0)
            return half * 48 + ((other + xl) & 1) * 24 + inner - 24 * half

        order = picks(target, 96, 96)
        for dy in range(8):
            y_from = (y - dy + 8) % 8
            rows = jnp.concatenate([branch_landed[0, dy], branch_landed[1, dy]], axis=0)
            ordered = moved(order, rows)
            branch_kv[0, y_from] = ordered[:48]
            branch_kv[1, y_from] = ordered[48:]
        attend(
            branch_kv[0].reshape(BR, HD), branch_kv[1].reshape(BR, HD),
            lambda block: shown[block], True,
        )

    def turn_queries():
        loads[3].wait()
        for head in range(HEADS):
            flipped = jnp.transpose(queries[:, head * HD : head * HD + HD])
            scaled = flipped.astype(jnp.float32) * SCORE_SCALE
            coarse = scaled.astype(jnp.bfloat16)
            fine = (scaled - coarse.astype(jnp.float32)).astype(jnp.bfloat16)
            columns = slice((head % 2) * BR, (head % 2) * BR + BR)
            turned[head // 2, :HD, columns] = coarse
            turned[head // 2, HD:, columns] = fine

    def mark_ancestors():
        loads[2].wait()
        above = lax.broadcasted_iota(jnp.int32, (HD, HD), 0)
        along = lax.broadcasted_iota(jnp.int32, (HD, HD), 1)

        def links(up, down):
            return above + up * HD == parents[:, down * HD : down * HD + HD]

        def as_picks(wanted):
            return jnp.where(wanted, 1.0, 0.0).astype(jnp.bfloat16)

        within = [as_picks(jnp.logical_or(links(b, b), above == along)) for b in range(3)]
        for _ in range(7):
            within = [
                as_picks(jnp.dot(one, one, preferred_element_type=jnp.float32) > 0.5)
                for one in within
            ]
        step_one = moved(as_picks(links(0, 1)), within[1])
        step_two = moved(as_picks(links(1, 2)), within[2])
        zero_one = moved(within[0], step_one)
        blocks = {
            (0, 0): within[0], (1, 1): within[1], (2, 2): within[2],
            (0, 1): zero_one, (1, 2): moved(within[1], step_two), (0, 2): moved(zero_one, step_two),
        }
        for up in range(3):
            for down in range(3):
                if (up, down) in blocks:
                    mask = jnp.where(blocks[up, down].astype(jnp.float32) > 0.5, 0.0, DEAD)
                else:
                    mask = jnp.full((HD, HD), DEAD, jnp.float32)
                shown[up * HD : up * HD + HD, down * HD : down * HD + HD] = mask

    lax.fori_loop(2, 3, stage_and_send, 0)
    pass_on(0)
    lax.fori_loop(3, 4, stage_and_send, 0)
    landed[48] = staged[6, y]
    pass_on(1)
    hand_on(0)
    turn_queries()
    wait_bytes(branch_landed.at[0, 1:8], recv_r)
    pltpu.make_async_remote_copy(
        src_ref=branch_landed.at[0],
        dst_ref=branch_landed.at[1],
        send_sem=send_p,
        recv_sem=recv_p,
        device_id=near(0, 1, 0),
        device_id_type=MESH,
    ).start()
    mark_ancestors()
    pass_on(2)
    hand_on(1)
    attend_branch()
    pass_on(3)
    hand_on(2)
    attend_chunk(0)
    hand_on(3)
    attend_chunk(1)
    attend_chunk(2)
    attend_chunk(3)

    for head in range(HEADS):
        columns = slice((head % 2) * BR, (head % 2) * BR + BR)
        result = summed[head // 2, :, columns] * (1.0 / total[head // 2, :, columns])
        out[:, head * HD : head * HD + HD] = jnp.transpose(result.astype(jnp.bfloat16))

    wait_bytes(landed.at[1:64], send_a)
    wait_bytes(branch_landed.at[0, 1:8], send_r)
    wait_bytes(branch_landed.at[0], send_p)
    wait_bytes(keys_values.at[:, 0:5], send_b)
    wait_bytes(keys_values.at[:, 0:2], send_f)


def local(trunk_kv, slot_trees, trunk_len, parents, queries, branch_kv):
    smem = pl.BlockSpec(memory_space=pltpu.SMEM)
    hbm = pl.BlockSpec(memory_space=pltpu.HBM)
    bf16, f32 = jnp.bfloat16, jnp.float32
    attended = pl.pallas_call(
        kernel,
        out_shape=jax.ShapeDtypeStruct((BR, HEADS * HD), bf16),
        in_specs=[smem, smem, hbm, hbm, hbm, hbm],
        out_specs=pl.BlockSpec(memory_space=pltpu.VMEM),
        scratch_shapes=[
            pltpu.VMEM((TREES, 32, 256), bf16),
            pltpu.VMEM((192, 256), bf16),
            pltpu.VMEM((BR, HEADS * HD), bf16),
            pltpu.VMEM((1, BR), jnp.int32),
            pltpu.VMEM((128, 128), bf16),
            pltpu.VMEM((256, 256), bf16),
            pltpu.VMEM((8, 8, 16, 256), bf16),
            pltpu.VMEM((64, 16, 256), bf16),
            pltpu.VMEM((CHUNKS, 4, 64, 256), bf16),
            pltpu.VMEM((CHUNKS, 8, 64, 256), bf16),
            pltpu.VMEM((8, 48, HD), bf16),
            pltpu.VMEM((2, 8, 48, HD), bf16),
            pltpu.VMEM((2, 8, 48, HD), bf16),
            pltpu.VMEM((PAIRS, 2 * HD, WIDE), bf16),
            pltpu.VMEM((BR, BR), f32),
            pltpu.VMEM((PAIRS, 1, WIDE), f32),
            pltpu.VMEM((PAIRS, 1, WIDE), f32),
            pltpu.VMEM((PAIRS, HD, WIDE), f32),
            pltpu.VMEM((512, HD), f32),
            pltpu.VMEM((PAIRS, 512, WIDE), f32),
            pltpu.VMEM((PAIRS, 512, WIDE), bf16),
            pltpu.SemaphoreType.DMA((4,)),
            pltpu.SemaphoreType.DMA,
            pltpu.SemaphoreType.DMA((CHUNKS,)),
            pltpu.SemaphoreType.DMA,
            pltpu.SemaphoreType.DMA((CHUNKS,)),
            pltpu.SemaphoreType.DMA((CHUNKS,)),
            pltpu.SemaphoreType.DMA,
            pltpu.SemaphoreType.DMA((CHUNKS,)),
            pltpu.SemaphoreType.DMA,
            pltpu.SemaphoreType.DMA,
            pltpu.SemaphoreType.DMA,
            pltpu.SemaphoreType.DMA,
        ],
        compiler_params=pltpu.CompilerParams(
            collective_id=0, has_side_effects=True, vmem_limit_bytes=60 * 1024 * 1024
        ),
    )(
        slot_trees,
        trunk_len,
        trunk_kv.reshape(TREES, 32, 2 * HD),
        branch_kv.reshape(192, 2 * HD),
        queries.reshape(BR, HEADS * HD),
        parents,
    )
    return attended.reshape(1, BR, HEADS * HD)


def solution(mesh):
    in_specs = (
        P(None, ("leaf", "tensor"), None, None),
        P(),
        P(),
        P("leaf", None),
        P("leaf", None, "tensor"),
        P("leaf", "tensor", None, None),
    )
    out_specs = P("leaf", None, "tensor")
    return jax.shard_map(local, mesh=mesh, in_specs=in_specs, out_specs=out_specs, check_vma=False)
```

```python
import math

import jax
import jax.numpy as jnp
from jax import lax
from jax.experimental import pallas as pl
from jax.experimental.pallas import tpu as pltpu
from jax.sharding import PartitionSpec as P

MESH = pl.DeviceIdType.MESH

HD = 128
BR = 384
TREES = 32
HEADS = 4
PAIRS = 2
WIDE = 2 * BR
CHUNKS = 4
BLOCK = 64
DEAD = -1e30
SCORE_SCALE = math.log2(math.e) / math.sqrt(HD)


def by_distance():
    def steps(pair):
        return min(pair[0], 8 - pair[0]) + min(pair[1], 8 - pair[1])

    pairs = sorted(((dz, dy) for dz in range(8) for dy in range(8)), key=lambda pair: (steps(pair), pair))
    return pairs[16:32] + pairs[48:64] + pairs[32:48] + pairs[15:0:-1] + pairs[:1]


PLANE = by_distance()


def picks(target, rows, columns):
    row = lax.broadcasted_iota(jnp.int32, (rows, columns), 0)
    column = lax.broadcasted_iota(jnp.int32, (rows, columns), 1)
    return jnp.where(row == target(column), 1.0, 0.0).astype(jnp.bfloat16)


def moved(order, rows):
    return jnp.dot(order, rows, preferred_element_type=jnp.float32).astype(jnp.bfloat16)


def kernel(
    slots_hbm, lengths_hbm, trunk_hbm, branch_hbm, queries_hbm, parents_hbm,
    out,
    slots, lengths, trunk, branch, queries, parents, pick_head, pick_target,
    staged, landed, sorted_rows, keys_values, branch_staged, branch_landed, branch_kv,
    turned, shown, top, total, summed, dead, raw, rounded, result,
    load, send_a, recv_a, send_b, recv_b, send_r, recv_r, send_p, recv_p, store,
):
    leaf = lax.axis_index("leaf")
    tensor = lax.axis_index("tensor")
    xh, z, c = leaf // 16, (leaf // 2) % 8, leaf % 2
    y, xl = tensor // 2, tensor % 2

    def place(xh, z, c, y, xl):
        return ((xh * 8 + z) * 2 + c, y * 2 + xl)

    def near(a, d, b):
        return place((xh + a) % 2, z, (c + b) % 2, y, (xl + d) % 2)

    barrier = pltpu.get_barrier_semaphore()
    ring = ((1, 0, 0), (1, 0, 1), (1, 1, 0), (1, 1, 1), (0, 1, 0), (0, 1, 1), (0, 0, 1))

    def signal(where):
        pl.semaphore_signal(barrier, inc=1, device_id=where, device_id_type=MESH)

    def greet(step, _):
        signal(place(xh, (z + step // 8) % 8, c, (y + step % 8) % 8, xl))
        return 0

    loads = [
        pltpu.make_async_copy(there, here, load.at[which])
        for which, (there, here) in enumerate(
            [
                (slots_hbm, slots), (trunk_hbm, trunk), (lengths_hbm, lengths),
                (branch_hbm, branch), (parents_hbm, parents), (queries_hbm, queries),
            ]
        )
    ]
    for one in loads:
        one.start()
    lax.fori_loop(1, 64, greet, 0)
    for flips in ring:
        signal(near(*flips))

    pick_head[...] = picks(
        lambda i: (i & 7) * 16 + (i >> 5) * 4 + ((i >> 3) & 3), 128, 128
    )
    pick_target[...] = picks(
        lambda i: ((i >> 2) & 3) * 64 + (i >> 4) * 4 + (i & 3), 256, 256
    )

    def stage(dz):
        z_to = (z + dz) % 8
        rows = jnp.concatenate(
            [trunk[slots[((q // 2) * 8 + z_to) * 2 + q % 2]] for q in range(4)], axis=0
        )
        ordered = moved(pick_head[...], rows)
        for head in range(8):
            staged[dz, head] = ordered[head * 16 : head * 16 + 16]

    def send_plane(chunk):
        for at in range(chunk * 16, chunk * 16 + 16):
            dz, dy = PLANE[at]
            if dz or dy:
                y_to = (y + dy) % 8
                pltpu.make_async_remote_copy(
                    src_ref=staged.at[dz, y_to],
                    dst_ref=landed.at[at],
                    send_sem=send_a,
                    recv_sem=recv_a.at[chunk],
                    device_id=place(xh, (z + dz) % 8, c, y_to, xl),
                    device_id_type=MESH,
                ).start()

    loads[0].wait()
    loads[1].wait()
    for dz in range(8):
        stage(dz)
    pl.semaphore_wait(barrier, 63 + len(ring))
    send_plane(0)

    loads[3].wait()

    def branch_target(i):
        half = jnp.where(i >= 192, 1, 0)
        inner = i - 192 * half
        return (inner & 7) * 48 + half * 24 + (inner >> 3)

    rows = jnp.concatenate([branch[:, :HD], branch[:, HD:]], axis=0)
    ordered = moved(picks(branch_target, 384, 384), rows)
    for head in range(8):
        branch_staged[head] = ordered[head * 48 : head * 48 + 48]
    for dy in (4, 3, 5, 2, 6, 1, 7):
        y_to = (y + dy) % 8
        pltpu.make_async_remote_copy(
            src_ref=branch_staged.at[y_to],
            dst_ref=branch_landed.at[0, dy],
            send_sem=send_r,
            recv_sem=recv_r,
            device_id=place(xh, z, c, y_to, xl),
            device_id_type=MESH,
        ).start()
    branch_landed[0, 0] = branch_staged[y]

    def wait_bytes(ref, sem):
        pltpu.make_async_copy(ref, ref, sem).wait()

    def pass_on(chunk):
        first = chunk * 16
        wait_bytes(landed.at[first : first + (15 if chunk == 3 else 16)], recv_a.at[chunk])
        rows = landed[first : first + 16].reshape(256, 256)
        ordered = moved(pick_target[...], rows)
        for target in range(4):
            sorted_rows[chunk, target] = ordered[target * 64 : target * 64 + 64]
        for a, d, b in ring:
            target = ((xh + a) % 2) * 2 + (c + b) % 2
            pltpu.make_async_remote_copy(
                src_ref=sorted_rows.at[chunk, target],
                dst_ref=keys_values.at[chunk, a * 4 + d * 2 + b],
                send_sem=send_b,
                recv_sem=recv_b.at[chunk],
                device_id=near(a, d, b),
                device_id_type=MESH,
            ).start()
        keys_values[chunk, 0] = sorted_rows[chunk, xh * 2 + c]

    def attend(keys, values, mask_rows, first):
        count = keys.shape[0]
        keys = jnp.concatenate([keys, keys], axis=1)
        values = jnp.transpose(values)
        blocks = [slice(at, at + BLOCK) for at in range(0, count, BLOCK)]
        for pair in range(PAIRS):
            raw[pair, :count] = jnp.dot(keys, turned[pair], preferred_element_type=jnp.float32)
        for pair in range(PAIRS):
            fades = []
            for half in range(2):
                columns = slice(half * BR, half * BR + BR)
                best = None if first else top[pair, :, columns]
                for block in blocks:
                    scores = raw[pair, block, columns] + mask_rows(block)
                    highest = jnp.max(scores, axis=0, keepdims=True)
                    best = highest if best is None else jnp.maximum(best, highest)
                weight_sum = None
                for block in blocks:
                    weights = jnp.exp2(raw[pair, block, columns] + mask_rows(block) - best)
                    part = jnp.sum(weights, axis=0, keepdims=True)
                    weight_sum = part if weight_sum is None else weight_sum + part
                    rounded[pair, block, columns] = weights.astype(jnp.bfloat16)
                if not first:
                    fades.append(jnp.exp2(top[pair, :, columns] - best))
                    weight_sum = total[pair, :, columns] * fades[half] + weight_sum
                total[pair, :, columns] = weight_sum
                top[pair, :, columns] = best
            product = jnp.dot(
                values, rounded[pair, :count], preferred_element_type=jnp.float32
            )
            for half in range(2):
                columns = slice(half * BR, half * BR + BR)
                if first:
                    summed[pair, :, columns] = product[:, columns]
                else:
                    summed[pair, :, columns] = (
                        summed[pair, :, columns] * fades[half] + product[:, columns]
                    )

    def attend_chunk(chunk):
        if chunk == 0:
            loads[2].wait()
        wait_bytes(keys_values.at[chunk, 1:8], recv_b.at[chunk])
        both = keys_values[chunk].reshape(512, 256)
        row = lax.broadcasted_iota(jnp.int32, (64, HD), 0)
        inner = row & 3
        for at in range(16):
            dz, dy = PLANE[chunk * 16 + at]
            start = ((z - dz + 8) % 8) * 128 + ((y - dy + 8) % 8) * 8
            inner = inner + jnp.where((row >> 2) == at, start, 0)
        outer = [
            (((xh + a) % 2) * 16 + (c + b) % 2) * 64 + ((xl + d) % 2) * 4
            for a in range(2) for d in range(2) for b in range(2)
        ]
        position = jnp.concatenate([inner + start for start in outer], axis=0)
        dead[...] = jnp.where(position < lengths[slots[leaf]], 0.0, DEAD)
        attend(
            both[:, :HD], both[:, HD:],
            lambda block: jnp.concatenate([dead[block]] * (BR // HD), axis=1), False,
        )

    def attend_branch():
        wait_bytes(branch_landed.at[1], recv_p)

        def target(i):
            other = jnp.where(i >= 48, 1, 0)
            inner = i - 48 * other
            half = jnp.where(inner >= 24, 1, 0)
            return half * 48 + ((other + xl) & 1) * 24 + inner - 24 * half

        order = picks(target, 96, 96)
        for dy in range(8):
            y_from = (y - dy + 8) % 8
            rows = jnp.concatenate([branch_landed[0, dy], branch_landed[1, dy]], axis=0)
            ordered = moved(order, rows)
            branch_kv[0, y_from] = ordered[:48]
            branch_kv[1, y_from] = ordered[48:]
        attend(
            branch_kv[0].reshape(BR, HD), branch_kv[1].reshape(BR, HD),
            lambda block: shown[block], True,
        )

    def turn_queries():
        loads[5].wait()
        for head in range(HEADS):
            flipped = jnp.transpose(queries[:, head * HD : head * HD + HD])
            scaled = flipped.astype(jnp.float32) * SCORE_SCALE
            coarse = scaled.astype(jnp.bfloat16)
            fine = (scaled - coarse.astype(jnp.float32)).astype(jnp.bfloat16)
            columns = slice((head % 2) * BR, (head % 2) * BR + BR)
            turned[head // 2, :HD, columns] = coarse
            turned[head // 2, HD:, columns] = fine

    def mark_ancestors():
        loads[4].wait()
        above = lax.broadcasted_iota(jnp.int32, (HD, HD), 0)
        along = lax.broadcasted_iota(jnp.int32, (HD, HD), 1)

        def links(up, down):
            return above + up * HD == parents[:, down * HD : down * HD + HD]

        def as_picks(wanted):
            return jnp.where(wanted, 1.0, 0.0).astype(jnp.bfloat16)

        within = [as_picks(jnp.logical_or(links(b, b), above == along)) for b in range(3)]
        for _ in range(7):
            within = [
                as_picks(jnp.dot(one, one, preferred_element_type=jnp.float32) > 0.5)
                for one in within
            ]
        step_one = moved(as_picks(links(0, 1)), within[1])
        step_two = moved(as_picks(links(1, 2)), within[2])
        zero_one = moved(within[0], step_one)
        blocks = {
            (0, 0): within[0], (1, 1): within[1], (2, 2): within[2],
            (0, 1): zero_one, (1, 2): moved(within[1], step_two), (0, 2): moved(zero_one, step_two),
        }
        for up in range(3):
            for down in range(3):
                if (up, down) in blocks:
                    mask = jnp.where(blocks[up, down].astype(jnp.float32) > 0.5, 0.0, DEAD)
                else:
                    mask = jnp.full((HD, HD), DEAD, jnp.float32)
                shown[up * HD : up * HD + HD, down * HD : down * HD + HD] = mask

    def hand_branch():
        wait_bytes(branch_landed.at[0, 1:8], recv_r)
        pltpu.make_async_remote_copy(
            src_ref=branch_landed.at[0],
            dst_ref=branch_landed.at[1],
            send_sem=send_p,
            recv_sem=recv_p,
            device_id=near(0, 1, 0),
            device_id_type=MESH,
        ).start()

    send_plane(1)
    send_plane(2)
    pass_on(0)
    send_plane(3)
    landed[63] = staged[0, y]
    turn_queries()
    pass_on(1)
    hand_branch()
    mark_ancestors()
    pass_on(2)
    attend_branch()
    pass_on(3)
    attend_chunk(0)
    attend_chunk(1)
    attend_chunk(2)
    attend_chunk(3)

    stores = []
    for head in range(HEADS):
        columns = slice((head % 2) * BR, (head % 2) * BR + BR)
        lanes = slice(head * HD, head * HD + HD)
        normal = summed[head // 2, :, columns] * (1.0 / total[head // 2, :, columns])
        result[:, lanes] = jnp.transpose(normal.astype(jnp.bfloat16))
        stores.append(pltpu.make_async_copy(result.at[:, lanes], out.at[:, lanes], store.at[head]))
        stores[-1].start()
    for one in stores:
        one.wait()

    wait_bytes(landed.at[0:63], send_a)
    wait_bytes(branch_landed.at[0, 1:8], send_r)
    wait_bytes(branch_landed.at[0], send_p)
    wait_bytes(keys_values.at[:, 1:8], send_b)


def local(trunk_kv, slot_trees, trunk_len, parents, queries, branch_kv):
    hbm = pl.BlockSpec(memory_space=pltpu.HBM)
    bf16, f32 = jnp.bfloat16, jnp.float32
    attended = pl.pallas_call(
        kernel,
        out_shape=jax.ShapeDtypeStruct((BR, HEADS * HD), bf16),
        in_specs=[hbm] * 6,
        out_specs=hbm,
        scratch_shapes=[
            pltpu.SMEM((TREES,), jnp.int32),
            pltpu.SMEM((TREES,), jnp.int32),
            pltpu.VMEM((TREES, 32, 256), bf16),
            pltpu.VMEM((192, 256), bf16),
            pltpu.VMEM((BR, HEADS * HD), bf16),
            pltpu.VMEM((1, BR), jnp.int32),
            pltpu.VMEM((128, 128), bf16),
            pltpu.VMEM((256, 256), bf16),
            pltpu.VMEM((8, 8, 16, 256), bf16),
            pltpu.VMEM((64, 16, 256), bf16),
            pltpu.VMEM((CHUNKS, 4, 64, 256), bf16),
            pltpu.VMEM((CHUNKS, 8, 64, 256), bf16),
            pltpu.VMEM((8, 48, HD), bf16),
            pltpu.VMEM((2, 8, 48, HD), bf16),
            pltpu.VMEM((2, 8, 48, HD), bf16),
            pltpu.VMEM((PAIRS, 2 * HD, WIDE), bf16),
            pltpu.VMEM((BR, BR), f32),
            pltpu.VMEM((PAIRS, 1, WIDE), f32),
            pltpu.VMEM((PAIRS, 1, WIDE), f32),
            pltpu.VMEM((PAIRS, HD, WIDE), f32),
            pltpu.VMEM((512, HD), f32),
            pltpu.VMEM((PAIRS, 512, WIDE), f32),
            pltpu.VMEM((PAIRS, 512, WIDE), bf16),
            pltpu.VMEM((BR, HEADS * HD), bf16),
            pltpu.SemaphoreType.DMA((6,)),
            pltpu.SemaphoreType.DMA,
            pltpu.SemaphoreType.DMA((CHUNKS,)),
            pltpu.SemaphoreType.DMA,
            pltpu.SemaphoreType.DMA((CHUNKS,)),
            pltpu.SemaphoreType.DMA,
            pltpu.SemaphoreType.DMA,
            pltpu.SemaphoreType.DMA,
            pltpu.SemaphoreType.DMA,
            pltpu.SemaphoreType.DMA((HEADS,)),
        ],
        compiler_params=pltpu.CompilerParams(
            collective_id=0, has_side_effects=True, vmem_limit_bytes=60 * 1024 * 1024
        ),
    )(
        slot_trees,
        trunk_len,
        trunk_kv.reshape(TREES, 32, 2 * HD),
        branch_kv.reshape(192, 2 * HD),
        queries.reshape(BR, HEADS * HD),
        parents,
    )
    return attended.reshape(1, BR, HEADS * HD)


def solution(mesh):
    in_specs = (
        P(None, ("leaf", "tensor"), None, None),
        P(),
        P(),
        P("leaf", None),
        P("leaf", None, "tensor"),
        P("leaf", "tensor", None, None),
    )
    out_specs = P("leaf", None, "tensor")
    return jax.shard_map(local, mesh=mesh, in_specs=in_specs, out_specs=out_specs, check_vma=False)
```

```python
import math

import jax
import jax.numpy as jnp
from jax import lax
from jax.experimental import pallas as pl
from jax.experimental.pallas import tpu as pltpu
from jax.sharding import PartitionSpec as P

MESH = pl.DeviceIdType.MESH

HD = 128
BR = 384
TREES = 32
HEADS = 4
PAIRS = 2
WIDE = 2 * BR
CHUNKS = 4
BLOCK = 64
DEAD = -1e30
SCORE_SCALE = math.log2(math.e) / math.sqrt(HD)


def by_distance():
    def steps(pair):
        return min(pair[0], 8 - pair[0]) + min(pair[1], 8 - pair[1])

    ways = (4, 3, 5, 2, 6, 1, 7)
    first = [(0, dy) for dy in ways] + [(dz, 0) for dz in ways]
    others = sorted(((dz, dy) for dz in ways for dy in ways), key=lambda pair: -steps(pair))
    return first + others + [(0, 0)]


PLANE = by_distance()


def picks(target, rows, columns):
    row = lax.broadcasted_iota(jnp.int32, (rows, columns), 0)
    column = lax.broadcasted_iota(jnp.int32, (rows, columns), 1)
    return jnp.where(row == target(column), 1.0, 0.0).astype(jnp.bfloat16)


def moved(order, rows):
    return jnp.dot(order, rows, preferred_element_type=jnp.float32).astype(jnp.bfloat16)


def kernel(
    slots_hbm, lengths_hbm, trunk_hbm, branch_hbm, queries_hbm, parents_hbm,
    out,
    slots, lengths, trunk, branch, queries, parents, pick_head, pick_target,
    staged, landed, sorted_rows, keys_values, branch_staged, branch_landed, branch_kv,
    turned, shown, top, total, summed, dead, raw, rounded, result,
    load, send_a, recv_a, send_b, recv_b, send_r, recv_r, send_p, recv_p, store, rows_in,
):
    leaf = lax.axis_index("leaf")
    tensor = lax.axis_index("tensor")
    xh, z, c = leaf // 16, (leaf // 2) % 8, leaf % 2
    y, xl = tensor // 2, tensor % 2

    def place(xh, z, c, y, xl):
        return ((xh * 8 + z) * 2 + c, y * 2 + xl)

    def near(a, d, b):
        return place((xh + a) % 2, z, (c + b) % 2, y, (xl + d) % 2)

    barrier = pltpu.get_barrier_semaphore()
    ring = ((1, 0, 0), (1, 0, 1), (1, 1, 0), (1, 1, 1), (0, 1, 0), (0, 1, 1), (0, 0, 1))

    def signal(where):
        pl.semaphore_signal(barrier, inc=1, device_id=where, device_id_type=MESH)

    for step in range(1, 8):
        signal(place(xh, z, c, (y + step) % 8, xl))
        signal(place(xh, (z + step) % 8, c, y, xl))
    for flips in ring:
        signal(near(*flips))

    loads = [
        pltpu.make_async_copy(there, here, load.at[which])
        for which, (there, here) in enumerate(
            [
                (slots_hbm, slots), (trunk_hbm, trunk), (lengths_hbm, lengths),
                (branch_hbm, branch), (parents_hbm, parents), (queries_hbm, queries),
            ]
        )
    ]
    for one in loads:
        one.start()
    pick_head[...] = picks(
        lambda i: (i & 7) * 16 + (i >> 5) * 4 + ((i >> 3) & 3), 128, 128
    )
    pick_target[...] = picks(
        lambda i: ((i >> 2) & 3) * 64 + (i >> 4) * 4 + (i & 3), 256, 256
    )

    def stage(dz):
        z_to = (z + dz) % 8
        rows = jnp.concatenate(
            [trunk[slots[((q // 2) * 8 + z_to) * 2 + q % 2]] for q in range(4)], axis=0
        )
        ordered = moved(pick_head[...], rows)
        for head in range(8):
            staged[dz, head] = ordered[head * 16 : head * 16 + 16]

    def send_plane(first, end):
        for at in range(first, end):
            dz, dy = PLANE[at]
            if dz or dy:
                y_to = (y + dy) % 8
                pltpu.make_async_remote_copy(
                    src_ref=staged.at[dz, y_to],
                    dst_ref=landed.at[at],
                    send_sem=send_a,
                    recv_sem=recv_a.at[at // 16],
                    device_id=place(xh, (z + dz) % 8, c, y_to, xl),
                    device_id_type=MESH,
                ).start()

    loads[0].wait()
    loads[1].wait()
    stage(0)
    pl.semaphore_wait(barrier, 14 + len(ring))
    for step in range(1, 8):
        pl.semaphore_signal(
            rows_in, inc=1, device_id=place(xh, (z + step) % 8, c, y, xl), device_id_type=MESH
        )
    send_plane(0, 7)
    for at in range(7, 14):
        stage(PLANE[at][0])
        send_plane(at, at + 1)
    pl.semaphore_wait(rows_in, 7)
    send_plane(14, 16)

    loads[3].wait()

    def branch_target(i):
        half = jnp.where(i >= 192, 1, 0)
        inner = i - 192 * half
        return (inner & 7) * 48 + half * 24 + (inner >> 3)

    rows = jnp.concatenate([branch[:, :HD], branch[:, HD:]], axis=0)
    ordered = moved(picks(branch_target, 384, 384), rows)
    for head in range(8):
        branch_staged[head] = ordered[head * 48 : head * 48 + 48]
    for dy in (4, 3, 5, 2, 6, 1, 7):
        y_to = (y + dy) % 8
        pltpu.make_async_remote_copy(
            src_ref=branch_staged.at[y_to],
            dst_ref=branch_landed.at[0, dy],
            send_sem=send_r,
            recv_sem=recv_r,
            device_id=place(xh, z, c, y_to, xl),
            device_id_type=MESH,
        ).start()
    branch_landed[0, 0] = branch_staged[y]

    def wait_bytes(ref, sem):
        pltpu.make_async_copy(ref, ref, sem).wait()

    def pass_on(chunk):
        first = chunk * 16
        wait_bytes(landed.at[first : first + (15 if chunk == 3 else 16)], recv_a.at[chunk])
        rows = landed[first : first + 16].reshape(256, 256)
        ordered = moved(pick_target[...], rows)
        for target in range(4):
            sorted_rows[chunk, target] = ordered[target * 64 : target * 64 + 64]
        for a, d, b in ring:
            target = ((xh + a) % 2) * 2 + (c + b) % 2
            pltpu.make_async_remote_copy(
                src_ref=sorted_rows.at[chunk, target],
                dst_ref=keys_values.at[chunk, a * 4 + d * 2 + b],
                send_sem=send_b,
                recv_sem=recv_b.at[chunk],
                device_id=near(a, d, b),
                device_id_type=MESH,
            ).start()
        keys_values[chunk, 0] = sorted_rows[chunk, xh * 2 + c]

    def attend(keys, values, mask_rows, first):
        count = keys.shape[0]
        keys = jnp.concatenate([keys, keys], axis=1)
        values = jnp.transpose(values)
        blocks = [slice(at, at + BLOCK) for at in range(0, count, BLOCK)]
        for pair in range(PAIRS):
            raw[pair, :count] = jnp.dot(keys, turned[pair], preferred_element_type=jnp.float32)
        for pair in range(PAIRS):
            fades = []
            for half in range(2):
                columns = slice(half * BR, half * BR + BR)
                best = None if first else top[pair, :, columns]
                for block in blocks:
                    scores = raw[pair, block, columns] + mask_rows(block)
                    highest = jnp.max(scores, axis=0, keepdims=True)
                    best = highest if best is None else jnp.maximum(best, highest)
                weight_sum = None
                for block in blocks:
                    weights = jnp.exp2(raw[pair, block, columns] + mask_rows(block) - best)
                    part = jnp.sum(weights, axis=0, keepdims=True)
                    weight_sum = part if weight_sum is None else weight_sum + part
                    rounded[pair, block, columns] = weights.astype(jnp.bfloat16)
                if not first:
                    fades.append(jnp.exp2(top[pair, :, columns] - best))
                    weight_sum = total[pair, :, columns] * fades[half] + weight_sum
                total[pair, :, columns] = weight_sum
                top[pair, :, columns] = best
            product = jnp.dot(
                values, rounded[pair, :count], preferred_element_type=jnp.float32
            )
            for half in range(2):
                columns = slice(half * BR, half * BR + BR)
                if first:
                    summed[pair, :, columns] = product[:, columns]
                else:
                    summed[pair, :, columns] = (
                        summed[pair, :, columns] * fades[half] + product[:, columns]
                    )

    def attend_chunk(chunk):
        if chunk == 0:
            loads[2].wait()
        wait_bytes(keys_values.at[chunk, 1:8], recv_b.at[chunk])
        both = keys_values[chunk].reshape(512, 256)
        row = lax.broadcasted_iota(jnp.int32, (64, HD), 0)
        inner = row & 3
        for at in range(16):
            dz, dy = PLANE[chunk * 16 + at]
            start = ((z - dz + 8) % 8) * 128 + ((y - dy + 8) % 8) * 8
            inner = inner + jnp.where((row >> 2) == at, start, 0)
        outer = [
            (((xh + a) % 2) * 16 + (c + b) % 2) * 64 + ((xl + d) % 2) * 4
            for a in range(2) for d in range(2) for b in range(2)
        ]
        position = jnp.concatenate([inner + start for start in outer], axis=0)
        dead[...] = jnp.where(position < lengths[slots[leaf]], 0.0, DEAD)
        attend(
            both[:, :HD], both[:, HD:],
            lambda block: jnp.concatenate([dead[block]] * (BR // HD), axis=1), False,
        )

    def attend_branch():
        wait_bytes(branch_landed.at[1], recv_p)

        def target(i):
            other = jnp.where(i >= 48, 1, 0)
            inner = i - 48 * other
            half = jnp.where(inner >= 24, 1, 0)
            return half * 48 + ((other + xl) & 1) * 24 + inner - 24 * half

        order = picks(target, 96, 96)
        for dy in range(8):
            y_from = (y - dy + 8) % 8
            rows = jnp.concatenate([branch_landed[0, dy], branch_landed[1, dy]], axis=0)
            ordered = moved(order, rows)
            branch_kv[0, y_from] = ordered[:48]
            branch_kv[1, y_from] = ordered[48:]
        attend(
            branch_kv[0].reshape(BR, HD), branch_kv[1].reshape(BR, HD),
            lambda block: shown[block], True,
        )

    def turn_queries():
        loads[5].wait()
        for head in range(HEADS):
            flipped = jnp.transpose(queries[:, head * HD : head * HD + HD])
            scaled = flipped.astype(jnp.float32) * SCORE_SCALE
            coarse = scaled.astype(jnp.bfloat16)
            fine = (scaled - coarse.astype(jnp.float32)).astype(jnp.bfloat16)
            columns = slice((head % 2) * BR, (head % 2) * BR + BR)
            turned[head // 2, :HD, columns] = coarse
            turned[head // 2, HD:, columns] = fine

    def mark_ancestors():
        loads[4].wait()
        above = lax.broadcasted_iota(jnp.int32, (HD, HD), 0)
        along = lax.broadcasted_iota(jnp.int32, (HD, HD), 1)

        def links(up, down):
            return above + up * HD == parents[:, down * HD : down * HD + HD]

        def as_picks(wanted):
            return jnp.where(wanted, 1.0, 0.0).astype(jnp.bfloat16)

        within = [as_picks(jnp.logical_or(links(b, b), above == along)) for b in range(3)]
        for _ in range(7):
            within = [
                as_picks(jnp.dot(one, one, preferred_element_type=jnp.float32) > 0.5)
                for one in within
            ]
        step_one = moved(as_picks(links(0, 1)), within[1])
        step_two = moved(as_picks(links(1, 2)), within[2])
        zero_one = moved(within[0], step_one)
        blocks = {
            (0, 0): within[0], (1, 1): within[1], (2, 2): within[2],
            (0, 1): zero_one, (1, 2): moved(within[1], step_two), (0, 2): moved(zero_one, step_two),
        }
        for up in range(3):
            for down in range(3):
                if (up, down) in blocks:
                    mask = jnp.where(blocks[up, down].astype(jnp.float32) > 0.5, 0.0, DEAD)
                else:
                    mask = jnp.full((HD, HD), DEAD, jnp.float32)
                shown[up * HD : up * HD + HD, down * HD : down * HD + HD] = mask

    def hand_branch():
        wait_bytes(branch_landed.at[0, 1:8], recv_r)
        pltpu.make_async_remote_copy(
            src_ref=branch_landed.at[0],
            dst_ref=branch_landed.at[1],
            send_sem=send_p,
            recv_sem=recv_p,
            device_id=near(0, 1, 0),
            device_id_type=MESH,
        ).start()

    send_plane(16, 48)
    pass_on(0)
    send_plane(48, 64)
    landed[63] = staged[0, y]
    turn_queries()
    pass_on(1)
    hand_branch()
    mark_ancestors()
    pass_on(2)
    attend_branch()
    pass_on(3)
    attend_chunk(0)
    attend_chunk(1)
    attend_chunk(2)
    attend_chunk(3)

    stores = []
    for head in range(HEADS):
        columns = slice((head % 2) * BR, (head % 2) * BR + BR)
        lanes = slice(head * HD, head * HD + HD)
        normal = summed[head // 2, :, columns] * (1.0 / total[head // 2, :, columns])
        result[:, lanes] = jnp.transpose(normal.astype(jnp.bfloat16))
        stores.append(pltpu.make_async_copy(result.at[:, lanes], out.at[:, lanes], store.at[head]))
        stores[-1].start()
    for one in stores:
        one.wait()

    wait_bytes(landed.at[0:63], send_a)
    wait_bytes(branch_landed.at[0, 1:8], send_r)
    wait_bytes(branch_landed.at[0], send_p)
    wait_bytes(keys_values.at[:, 1:8], send_b)


def local(trunk_kv, slot_trees, trunk_len, parents, queries, branch_kv):
    hbm = pl.BlockSpec(memory_space=pltpu.HBM)
    bf16, f32 = jnp.bfloat16, jnp.float32
    attended = pl.pallas_call(
        kernel,
        out_shape=jax.ShapeDtypeStruct((BR, HEADS * HD), bf16),
        in_specs=[hbm] * 6,
        out_specs=hbm,
        scratch_shapes=[
            pltpu.SMEM((TREES,), jnp.int32),
            pltpu.SMEM((TREES,), jnp.int32),
            pltpu.VMEM((TREES, 32, 256), bf16),
            pltpu.VMEM((192, 256), bf16),
            pltpu.VMEM((BR, HEADS * HD), bf16),
            pltpu.VMEM((1, BR), jnp.int32),
            pltpu.VMEM((128, 128), bf16),
            pltpu.VMEM((256, 256), bf16),
            pltpu.VMEM((8, 8, 16, 256), bf16),
            pltpu.VMEM((64, 16, 256), bf16),
            pltpu.VMEM((CHUNKS, 4, 64, 256), bf16),
            pltpu.VMEM((CHUNKS, 8, 64, 256), bf16),
            pltpu.VMEM((8, 48, HD), bf16),
            pltpu.VMEM((2, 8, 48, HD), bf16),
            pltpu.VMEM((2, 8, 48, HD), bf16),
            pltpu.VMEM((PAIRS, 2 * HD, WIDE), bf16),
            pltpu.VMEM((BR, BR), f32),
            pltpu.VMEM((PAIRS, 1, WIDE), f32),
            pltpu.VMEM((PAIRS, 1, WIDE), f32),
            pltpu.VMEM((PAIRS, HD, WIDE), f32),
            pltpu.VMEM((512, HD), f32),
            pltpu.VMEM((PAIRS, 512, WIDE), f32),
            pltpu.VMEM((PAIRS, 512, WIDE), bf16),
            pltpu.VMEM((BR, HEADS * HD), bf16),
            pltpu.SemaphoreType.DMA((6,)),
            pltpu.SemaphoreType.DMA,
            pltpu.SemaphoreType.DMA((CHUNKS,)),
            pltpu.SemaphoreType.DMA,
            pltpu.SemaphoreType.DMA((CHUNKS,)),
            pltpu.SemaphoreType.DMA,
            pltpu.SemaphoreType.DMA,
            pltpu.SemaphoreType.DMA,
            pltpu.SemaphoreType.DMA,
            pltpu.SemaphoreType.DMA((HEADS,)),
            pltpu.SemaphoreType.REGULAR,
        ],
        compiler_params=pltpu.CompilerParams(
            collective_id=0, has_side_effects=True, vmem_limit_bytes=60 * 1024 * 1024
        ),
    )(
        slot_trees,
        trunk_len,
        trunk_kv.reshape(TREES, 32, 2 * HD),
        branch_kv.reshape(192, 2 * HD),
        queries.reshape(BR, HEADS * HD),
        parents,
    )
    return attended.reshape(1, BR, HEADS * HD)


def solution(mesh):
    in_specs = (
        P(None, ("leaf", "tensor"), None, None),
        P(),
        P(),
        P("leaf", None),
        P("leaf", None, "tensor"),
        P("leaf", "tensor", None, None),
    )
    out_specs = P("leaf", None, "tensor")
    return jax.shard_map(local, mesh=mesh, in_specs=in_specs, out_specs=out_specs, check_vma=False)
```

```python
import math

import jax
import jax.numpy as jnp
from jax import lax
from jax.experimental import pallas as pl
from jax.experimental.pallas import tpu as pltpu
from jax.sharding import PartitionSpec as P

MESH = pl.DeviceIdType.MESH

HD = 128
BR = 384
TREES = 32
HEADS = 4
PAIRS = 2
WIDE = 2 * BR
BOUNDS = (0, 16, 40, 56, 64)
CHUNKS = len(BOUNDS) - 1
WIDEST = 24 * 32
BLOCK = 64
DEAD = -1e30
SCORE_SCALE = math.log2(math.e) / math.sqrt(HD)


def by_distance():
    def steps(pair):
        return min(pair[0], 8 - pair[0]) + min(pair[1], 8 - pair[1])

    ways = (4, 3, 5, 2, 6, 1, 7)
    first = [(0, dy) for dy in ways] + [(dz, 0) for dz in ways]
    others = sorted(((dz, dy) for dz in ways for dy in ways), key=lambda pair: -steps(pair))
    return first + others + [(0, 0)]


PLANE = by_distance()


def picks(target, rows, columns):
    row = lax.broadcasted_iota(jnp.int32, (rows, columns), 0)
    column = lax.broadcasted_iota(jnp.int32, (rows, columns), 1)
    return jnp.where(row == target(column), 1.0, 0.0).astype(jnp.bfloat16)


def moved(order, rows):
    return jnp.dot(order, rows, preferred_element_type=jnp.float32).astype(jnp.bfloat16)


def kernel(
    slots_hbm, lengths_hbm, trunk_hbm, branch_hbm, queries_hbm, parents_hbm,
    out,
    slots, lengths, trunk, branch, queries, parents, pick_head, pick_target,
    staged, landed, sorted_rows, keys_values, branch_staged, branch_landed, branch_kv,
    turned, shown, top, total, summed, dead, raw, rounded, result,
    load, send_a, recv_a, send_b, recv_b, send_r, recv_r, send_p, recv_p, store, rows_in,
):
    leaf = lax.axis_index("leaf")
    tensor = lax.axis_index("tensor")
    xh, z, c = leaf // 16, (leaf // 2) % 8, leaf % 2
    y, xl = tensor // 2, tensor % 2

    def place(xh, z, c, y, xl):
        return ((xh * 8 + z) * 2 + c, y * 2 + xl)

    def near(a, d, b):
        return place((xh + a) % 2, z, (c + b) % 2, y, (xl + d) % 2)

    barrier = pltpu.get_barrier_semaphore()
    ring = ((1, 0, 0), (1, 0, 1), (1, 1, 0), (1, 1, 1), (0, 1, 0), (0, 1, 1), (0, 0, 1))

    def signal(where):
        pl.semaphore_signal(barrier, inc=1, device_id=where, device_id_type=MESH)

    for step in range(1, 8):
        signal(place(xh, z, c, (y + step) % 8, xl))
        signal(place(xh, (z + step) % 8, c, y, xl))
    for flips in ring:
        signal(near(*flips))

    loads = [
        pltpu.make_async_copy(there, here, load.at[which])
        for which, (there, here) in enumerate(
            [
                (slots_hbm, slots), (trunk_hbm, trunk), (lengths_hbm, lengths),
                (branch_hbm, branch), (parents_hbm, parents), (queries_hbm, queries),
            ]
        )
    ]
    for one in loads:
        one.start()
    pick_head[...] = picks(
        lambda i: (i & 7) * 16 + (i >> 5) * 4 + ((i >> 3) & 3), 128, 128
    )
    pick_target[...] = picks(
        lambda i: ((i >> 2) & 3) * 32 + (i >> 4) * 4 + (i & 3), 128, 128
    )

    def stage(dz):
        z_to = (z + dz) % 8
        rows = jnp.concatenate(
            [trunk[slots[((q // 2) * 8 + z_to) * 2 + q % 2]] for q in range(4)], axis=0
        )
        ordered = moved(pick_head[...], rows)
        for head in range(8):
            staged[dz, head] = ordered[head * 16 : head * 16 + 16]

    def send_plane(first, end):
        for at in range(first, end):
            dz, dy = PLANE[at]
            if dz or dy:
                y_to = (y + dy) % 8
                pltpu.make_async_remote_copy(
                    src_ref=staged.at[dz, y_to],
                    dst_ref=landed.at[at],
                    send_sem=send_a,
                    recv_sem=recv_a.at[sum(at >= bound for bound in BOUNDS[1:])],
                    device_id=place(xh, (z + dz) % 8, c, y_to, xl),
                    device_id_type=MESH,
                ).start()

    loads[0].wait()
    loads[1].wait()
    stage(0)
    pl.semaphore_wait(barrier, 14 + len(ring))
    for step in range(1, 8):
        pl.semaphore_signal(
            rows_in, inc=1, device_id=place(xh, (z + step) % 8, c, y, xl), device_id_type=MESH
        )
    send_plane(0, 7)
    for at in range(7, 14):
        stage(PLANE[at][0])
        send_plane(at, at + 1)
    pl.semaphore_wait(rows_in, 7)
    send_plane(14, 16)

    loads[3].wait()

    def branch_target(i):
        half = jnp.where(i >= 192, 1, 0)
        inner = i - 192 * half
        return (inner & 7) * 48 + half * 24 + (inner >> 3)

    rows = jnp.concatenate([branch[:, :HD], branch[:, HD:]], axis=0)
    ordered = moved(picks(branch_target, 384, 384), rows)
    for head in range(8):
        branch_staged[head] = ordered[head * 48 : head * 48 + 48]
    for dy in (4, 3, 5, 2, 6, 1, 7):
        y_to = (y + dy) % 8
        pltpu.make_async_remote_copy(
            src_ref=branch_staged.at[y_to],
            dst_ref=branch_landed.at[0, dy],
            send_sem=send_r,
            recv_sem=recv_r,
            device_id=place(xh, z, c, y_to, xl),
            device_id_type=MESH,
        ).start()
    branch_landed[0, 0] = branch_staged[y]

    def wait_bytes(ref, sem):
        pltpu.make_async_copy(ref, ref, sem).wait()

    def pass_on(chunk):
        first, end = BOUNDS[chunk], BOUNDS[chunk + 1]
        wait_bytes(landed.at[first : end - 1 if chunk == CHUNKS - 1 else end], recv_a.at[chunk])
        for at in range(first, end, 8):
            ordered = moved(pick_target[...], landed[at : at + 8].reshape(128, 256))
            for target in range(4):
                sorted_rows[target, at * 4 : at * 4 + 32] = ordered[target * 32 : target * 32 + 32]
        rows = slice(first * 4, end * 4)
        for a, d, b in ring:
            target = ((xh + a) % 2) * 2 + (c + b) % 2
            pltpu.make_async_remote_copy(
                src_ref=sorted_rows.at[target, rows],
                dst_ref=keys_values.at[a * 4 + d * 2 + b, rows],
                send_sem=send_b,
                recv_sem=recv_b.at[chunk],
                device_id=near(a, d, b),
                device_id_type=MESH,
            ).start()
        keys_values[0, rows] = sorted_rows[xh * 2 + c, rows]

    def attend(keys, values, mask_rows, first):
        count = keys.shape[0]
        keys = jnp.concatenate([keys, keys], axis=1)
        values = jnp.transpose(values)
        blocks = [slice(at, at + BLOCK) for at in range(0, count, BLOCK)]
        for pair in range(PAIRS):
            raw[pair, :count] = jnp.dot(keys, turned[pair], preferred_element_type=jnp.float32)
        for pair in range(PAIRS):
            fades = []
            for half in range(2):
                columns = slice(half * BR, half * BR + BR)
                best = None if first else top[pair, :, columns]
                for block in blocks:
                    scores = raw[pair, block, columns] + mask_rows(block)
                    highest = jnp.max(scores, axis=0, keepdims=True)
                    best = highest if best is None else jnp.maximum(best, highest)
                weight_sum = None
                for block in blocks:
                    weights = jnp.exp2(raw[pair, block, columns] + mask_rows(block) - best)
                    part = jnp.sum(weights, axis=0, keepdims=True)
                    weight_sum = part if weight_sum is None else weight_sum + part
                    rounded[pair, block, columns] = weights.astype(jnp.bfloat16)
                if not first:
                    fades.append(jnp.exp2(top[pair, :, columns] - best))
                    weight_sum = total[pair, :, columns] * fades[half] + weight_sum
                total[pair, :, columns] = weight_sum
                top[pair, :, columns] = best
            product = jnp.dot(
                values, rounded[pair, :count], preferred_element_type=jnp.float32
            )
            for half in range(2):
                columns = slice(half * BR, half * BR + BR)
                if first:
                    summed[pair, :, columns] = product[:, columns]
                else:
                    summed[pair, :, columns] = (
                        summed[pair, :, columns] * fades[half] + product[:, columns]
                    )

    def attend_chunk(chunk):
        if chunk == 0:
            loads[2].wait()
        first, end = BOUNDS[chunk], BOUNDS[chunk + 1]
        count = (end - first) * 32
        wait_bytes(keys_values.at[1:8, first * 4 : end * 4], recv_b.at[chunk])
        both = keys_values[:, first * 4 : end * 4].reshape(count, 256)
        row = lax.broadcasted_iota(jnp.int32, (count // 8, HD), 0)
        inner = row & 3
        for at in range(first, end):
            dz, dy = PLANE[at]
            start = ((z - dz + 8) % 8) * 128 + ((y - dy + 8) % 8) * 8
            inner = inner + jnp.where((row >> 2) == at - first, start, 0)
        outer = [
            (((xh + a) % 2) * 16 + (c + b) % 2) * 64 + ((xl + d) % 2) * 4
            for a in range(2) for d in range(2) for b in range(2)
        ]
        position = jnp.concatenate([inner + start for start in outer], axis=0)
        dead[:count] = jnp.where(position < lengths[slots[leaf]], 0.0, DEAD)
        attend(
            both[:, :HD], both[:, HD:],
            lambda block: jnp.concatenate([dead[block]] * (BR // HD), axis=1), False,
        )

    def attend_branch():
        wait_bytes(branch_landed.at[1], recv_p)

        def target(i):
            other = jnp.where(i >= 48, 1, 0)
            inner = i - 48 * other
            half = jnp.where(inner >= 24, 1, 0)
            return half * 48 + ((other + xl) & 1) * 24 + inner - 24 * half

        order = picks(target, 96, 96)
        for dy in range(8):
            y_from = (y - dy + 8) % 8
            rows = jnp.concatenate([branch_landed[0, dy], branch_landed[1, dy]], axis=0)
            ordered = moved(order, rows)
            branch_kv[0, y_from] = ordered[:48]
            branch_kv[1, y_from] = ordered[48:]
        attend(
            branch_kv[0].reshape(BR, HD), branch_kv[1].reshape(BR, HD),
            lambda block: shown[block], True,
        )

    def turn_queries():
        loads[5].wait()
        for head in range(HEADS):
            flipped = jnp.transpose(queries[:, head * HD : head * HD + HD])
            scaled = flipped.astype(jnp.float32) * SCORE_SCALE
            coarse = scaled.astype(jnp.bfloat16)
            fine = (scaled - coarse.astype(jnp.float32)).astype(jnp.bfloat16)
            columns = slice((head % 2) * BR, (head % 2) * BR + BR)
            turned[head // 2, :HD, columns] = coarse
            turned[head // 2, HD:, columns] = fine

    def mark_ancestors():
        loads[4].wait()
        above = lax.broadcasted_iota(jnp.int32, (HD, HD), 0)
        along = lax.broadcasted_iota(jnp.int32, (HD, HD), 1)

        def links(up, down):
            return above + up * HD == parents[:, down * HD : down * HD + HD]

        def as_picks(wanted):
            return jnp.where(wanted, 1.0, 0.0).astype(jnp.bfloat16)

        within = [as_picks(jnp.logical_or(links(b, b), above == along)) for b in range(3)]
        for _ in range(7):
            within = [
                as_picks(jnp.dot(one, one, preferred_element_type=jnp.float32) > 0.5)
                for one in within
            ]
        step_one = moved(as_picks(links(0, 1)), within[1])
        step_two = moved(as_picks(links(1, 2)), within[2])
        zero_one = moved(within[0], step_one)
        blocks = {
            (0, 0): within[0], (1, 1): within[1], (2, 2): within[2],
            (0, 1): zero_one, (1, 2): moved(within[1], step_two), (0, 2): moved(zero_one, step_two),
        }
        for up in range(3):
            for down in range(3):
                if (up, down) in blocks:
                    mask = jnp.where(blocks[up, down].astype(jnp.float32) > 0.5, 0.0, DEAD)
                else:
                    mask = jnp.full((HD, HD), DEAD, jnp.float32)
                shown[up * HD : up * HD + HD, down * HD : down * HD + HD] = mask

    def hand_branch():
        wait_bytes(branch_landed.at[0, 1:8], recv_r)
        pltpu.make_async_remote_copy(
            src_ref=branch_landed.at[0],
            dst_ref=branch_landed.at[1],
            send_sem=send_p,
            recv_sem=recv_p,
            device_id=near(0, 1, 0),
            device_id_type=MESH,
        ).start()

    send_plane(16, 48)
    pass_on(0)
    send_plane(48, 64)
    landed[63] = staged[0, y]
    turn_queries()
    pass_on(1)
    hand_branch()
    mark_ancestors()
    pass_on(2)
    attend_branch()
    pass_on(3)
    attend_chunk(0)
    attend_chunk(1)
    attend_chunk(2)
    attend_chunk(3)

    stores = []
    for head in range(HEADS):
        columns = slice((head % 2) * BR, (head % 2) * BR + BR)
        lanes = slice(head * HD, head * HD + HD)
        normal = summed[head // 2, :, columns] * (1.0 / total[head // 2, :, columns])
        result[:, lanes] = jnp.transpose(normal.astype(jnp.bfloat16))
        stores.append(pltpu.make_async_copy(result.at[:, lanes], out.at[:, lanes], store.at[head]))
        stores[-1].start()
    for one in stores:
        one.wait()

    wait_bytes(landed.at[0:63], send_a)
    wait_bytes(branch_landed.at[0, 1:8], send_r)
    wait_bytes(branch_landed.at[0], send_p)
    wait_bytes(keys_values.at[1:8], send_b)


def local(trunk_kv, slot_trees, trunk_len, parents, queries, branch_kv):
    hbm = pl.BlockSpec(memory_space=pltpu.HBM)
    bf16, f32 = jnp.bfloat16, jnp.float32
    attended = pl.pallas_call(
        kernel,
        out_shape=jax.ShapeDtypeStruct((BR, HEADS * HD), bf16),
        in_specs=[hbm] * 6,
        out_specs=hbm,
        scratch_shapes=[
            pltpu.SMEM((TREES,), jnp.int32),
            pltpu.SMEM((TREES,), jnp.int32),
            pltpu.VMEM((TREES, 32, 256), bf16),
            pltpu.VMEM((192, 256), bf16),
            pltpu.VMEM((BR, HEADS * HD), bf16),
            pltpu.VMEM((1, BR), jnp.int32),
            pltpu.VMEM((128, 128), bf16),
            pltpu.VMEM((128, 128), bf16),
            pltpu.VMEM((8, 8, 16, 256), bf16),
            pltpu.VMEM((64, 16, 256), bf16),
            pltpu.VMEM((4, 256, 256), bf16),
            pltpu.VMEM((8, 256, 256), bf16),
            pltpu.VMEM((8, 48, HD), bf16),
            pltpu.VMEM((2, 8, 48, HD), bf16),
            pltpu.VMEM((2, 8, 48, HD), bf16),
            pltpu.VMEM((PAIRS, 2 * HD, WIDE), bf16),
            pltpu.VMEM((BR, BR), f32),
            pltpu.VMEM((PAIRS, 1, WIDE), f32),
            pltpu.VMEM((PAIRS, 1, WIDE), f32),
            pltpu.VMEM((PAIRS, HD, WIDE), f32),
            pltpu.VMEM((WIDEST, HD), f32),
            pltpu.VMEM((PAIRS, WIDEST, WIDE), f32),
            pltpu.VMEM((PAIRS, WIDEST, WIDE), bf16),
            pltpu.VMEM((BR, HEADS * HD), bf16),
            pltpu.SemaphoreType.DMA((6,)),
            pltpu.SemaphoreType.DMA,
            pltpu.SemaphoreType.DMA((CHUNKS,)),
            pltpu.SemaphoreType.DMA,
            pltpu.SemaphoreType.DMA((CHUNKS,)),
            pltpu.SemaphoreType.DMA,
            pltpu.SemaphoreType.DMA,
            pltpu.SemaphoreType.DMA,
            pltpu.SemaphoreType.DMA,
            pltpu.SemaphoreType.DMA((HEADS,)),
            pltpu.SemaphoreType.REGULAR,
        ],
        compiler_params=pltpu.CompilerParams(
            collective_id=0, has_side_effects=True, vmem_limit_bytes=60 * 1024 * 1024
        ),
    )(
        slot_trees,
        trunk_len,
        trunk_kv.reshape(TREES, 32, 2 * HD),
        branch_kv.reshape(192, 2 * HD),
        queries.reshape(BR, HEADS * HD),
        parents,
    )
    return attended.reshape(1, BR, HEADS * HD)


def solution(mesh):
    in_specs = (
        P(None, ("leaf", "tensor"), None, None),
        P(),
        P(),
        P("leaf", None),
        P("leaf", None, "tensor"),
        P("leaf", "tensor", None, None),
    )
    out_specs = P("leaf", None, "tensor")
    return jax.shard_map(local, mesh=mesh, in_specs=in_specs, out_specs=out_specs, check_vma=False)
```

```python
import math

import jax
import jax.numpy as jnp
from jax import lax
from jax.experimental import pallas as pl
from jax.experimental.pallas import tpu as pltpu
from jax.sharding import PartitionSpec as P

MESH = pl.DeviceIdType.MESH

HD = 128
BR = 384
TREES = 32
HEADS = 4
PAIRS = 2
WIDE = 2 * BR
CHUNKS = 4
BLOCK = 64
DEAD = -1e30
SCORE_SCALE = math.log2(math.e) / math.sqrt(HD)


def by_distance():
    def steps(pair):
        return min(pair[0], 8 - pair[0]) + min(pair[1], 8 - pair[1])

    ways = (4, 3, 5, 2, 6, 1, 7)
    first = [(0, dy) for dy in ways] + [(dz, 0) for dz in ways]
    others = sorted(((dz, dy) for dz in ways for dy in ways), key=lambda pair: -steps(pair))
    return first + others + [(0, 0)]


PLANE = by_distance()


def picks(target, rows, columns):
    row = lax.broadcasted_iota(jnp.int32, (rows, columns), 0)
    column = lax.broadcasted_iota(jnp.int32, (rows, columns), 1)
    return jnp.where(row == target(column), 1.0, 0.0).astype(jnp.bfloat16)


def moved(order, rows):
    return jnp.dot(order, rows, preferred_element_type=jnp.float32).astype(jnp.bfloat16)


def kernel(
    slots_hbm, lengths_hbm, trunk_hbm, branch_hbm, queries_hbm, parents_hbm,
    out,
    slots, lengths, trunk, branch, queries, parents, pick_head, pick_target,
    staged, landed, sorted_rows, keys_values, branch_staged, branch_landed, branch_kv,
    turned, shown, top, total, summed, dead, raw, rounded, result,
    load, send_a, recv_a, send_b, recv_b, send_r, recv_r, send_p, recv_p, store, rows_in,
):
    leaf = lax.axis_index("leaf")
    tensor = lax.axis_index("tensor")
    xh, z, c = leaf // 16, (leaf // 2) % 8, leaf % 2
    y, xl = tensor // 2, tensor % 2

    def place(xh, z, c, y, xl):
        return ((xh * 8 + z) * 2 + c, y * 2 + xl)

    def near(a, d, b):
        return place((xh + a) % 2, z, (c + b) % 2, y, (xl + d) % 2)

    barrier = pltpu.get_barrier_semaphore()
    ring = ((1, 0, 0), (1, 0, 1), (1, 1, 0), (1, 1, 1), (0, 1, 0), (0, 1, 1), (0, 0, 1))

    def signal(where):
        pl.semaphore_signal(barrier, inc=1, device_id=where, device_id_type=MESH)

    for step in range(1, 8):
        signal(place(xh, z, c, (y + step) % 8, xl))
        signal(place(xh, (z + step) % 8, c, y, xl))
    for flips in ring:
        signal(near(*flips))

    loads = [
        pltpu.make_async_copy(there, here, load.at[which])
        for which, (there, here) in enumerate(
            [
                (slots_hbm, slots), (trunk_hbm, trunk), (lengths_hbm, lengths),
                (branch_hbm, branch), (parents_hbm, parents), (queries_hbm, queries),
            ]
        )
    ]
    for one in loads:
        one.start()
    pick_head[...] = picks(
        lambda i: (i & 7) * 16 + (i >> 5) * 4 + ((i >> 3) & 3), 128, 128
    )
    pick_target[...] = picks(
        lambda i: ((i >> 2) & 3) * 64 + (i >> 4) * 4 + (i & 3), 256, 256
    )

    def stage(dz):
        z_to = (z + dz) % 8
        rows = jnp.concatenate(
            [trunk[slots[((q // 2) * 8 + z_to) * 2 + q % 2]] for q in range(4)], axis=0
        )
        ordered = moved(pick_head[...], rows)
        for head in range(8):
            staged[dz, head] = ordered[head * 16 : head * 16 + 16]

    def send_plane(first, end):
        for at in range(first, end):
            dz, dy = PLANE[at]
            if dz or dy:
                y_to = (y + dy) % 8
                pltpu.make_async_remote_copy(
                    src_ref=staged.at[dz, y_to],
                    dst_ref=landed.at[at],
                    send_sem=send_a,
                    recv_sem=recv_a.at[at // 16],
                    device_id=place(xh, (z + dz) % 8, c, y_to, xl),
                    device_id_type=MESH,
                ).start()

    loads[0].wait()
    loads[1].wait()
    stage(0)
    pl.semaphore_wait(barrier, 14 + len(ring))
    for step in range(1, 8):
        pl.semaphore_signal(
            rows_in, inc=1, device_id=place(xh, (z + step) % 8, c, y, xl), device_id_type=MESH
        )
    send_plane(0, 7)
    for at in range(7, 14):
        stage(PLANE[at][0])
        send_plane(at, at + 1)
    pl.semaphore_wait(rows_in, 7)
    send_plane(14, 16)

    loads[3].wait()

    def branch_target(i):
        half = jnp.where(i >= 192, 1, 0)
        inner = i - 192 * half
        return (inner & 7) * 48 + half * 24 + (inner >> 3)

    rows = jnp.concatenate([branch[:, :HD], branch[:, HD:]], axis=0)
    ordered = moved(picks(branch_target, 384, 384), rows)
    for head in range(8):
        branch_staged[head] = ordered[head * 48 : head * 48 + 48]
    for dy in (4, 3, 5, 2, 6, 1, 7):
        y_to = (y + dy) % 8
        pltpu.make_async_remote_copy(
            src_ref=branch_staged.at[y_to],
            dst_ref=branch_landed.at[0, dy],
            send_sem=send_r,
            recv_sem=recv_r,
            device_id=place(xh, z, c, y_to, xl),
            device_id_type=MESH,
        ).start()
    branch_landed[0, 0] = branch_staged[y]

    def wait_bytes(ref, sem):
        pltpu.make_async_copy(ref, ref, sem).wait()

    def pass_on(chunk):
        first = chunk * 16
        wait_bytes(landed.at[first : first + (15 if chunk == 3 else 16)], recv_a.at[chunk])
        rows = landed[first : first + 16].reshape(256, 256)
        ordered = moved(pick_target[...], rows)
        for target in range(4):
            sorted_rows[chunk, target] = ordered[target * 64 : target * 64 + 64]
        for a, d, b in ring:
            target = ((xh + a) % 2) * 2 + (c + b) % 2
            pltpu.make_async_remote_copy(
                src_ref=sorted_rows.at[chunk, target],
                dst_ref=keys_values.at[chunk, a * 4 + d * 2 + b],
                send_sem=send_b,
                recv_sem=recv_b.at[chunk],
                device_id=near(a, d, b),
                device_id_type=MESH,
            ).start()
        keys_values[chunk, 0] = sorted_rows[chunk, xh * 2 + c]

    def attend(keys, values, mask_rows, first):
        count = keys.shape[0]
        keys = jnp.concatenate([keys, keys], axis=1)
        values = jnp.transpose(values)
        blocks = [slice(at, at + BLOCK) for at in range(0, count, BLOCK)]
        for pair in range(PAIRS):
            raw[pair, :count] = jnp.dot(keys, turned[pair], preferred_element_type=jnp.float32)
        for pair in range(PAIRS):
            fades = []
            for half in range(2):
                columns = slice(half * BR, half * BR + BR)
                best = None if first else top[pair, :, columns]
                for block in blocks:
                    scores = raw[pair, block, columns] + mask_rows(block)
                    highest = jnp.max(scores, axis=0, keepdims=True)
                    best = highest if best is None else jnp.maximum(best, highest)
                weight_sum = None
                for block in blocks:
                    weights = jnp.exp2(raw[pair, block, columns] + mask_rows(block) - best)
                    part = jnp.sum(weights, axis=0, keepdims=True)
                    weight_sum = part if weight_sum is None else weight_sum + part
                    rounded[pair, block, columns] = weights.astype(jnp.bfloat16)
                if not first:
                    fades.append(jnp.exp2(top[pair, :, columns] - best))
                    weight_sum = total[pair, :, columns] * fades[half] + weight_sum
                total[pair, :, columns] = weight_sum
                top[pair, :, columns] = best
            product = jnp.dot(
                values, rounded[pair, :count], preferred_element_type=jnp.float32
            )
            for half in range(2):
                columns = slice(half * BR, half * BR + BR)
                if first:
                    summed[pair, :, columns] = product[:, columns]
                else:
                    summed[pair, :, columns] = (
                        summed[pair, :, columns] * fades[half] + product[:, columns]
                    )

    def attend_chunk(chunk):
        if chunk == 0:
            loads[2].wait()
        wait_bytes(keys_values.at[chunk, 1:8], recv_b.at[chunk])
        both = keys_values[chunk].reshape(512, 256)
        row = lax.broadcasted_iota(jnp.int32, (64, HD), 0)
        inner = row & 3
        for at in range(16):
            dz, dy = PLANE[chunk * 16 + at]
            start = ((z - dz + 8) % 8) * 128 + ((y - dy + 8) % 8) * 8
            inner = inner + jnp.where((row >> 2) == at, start, 0)
        outer = [
            (((xh + a) % 2) * 16 + (c + b) % 2) * 64 + ((xl + d) % 2) * 4
            for a in range(2) for d in range(2) for b in range(2)
        ]
        position = jnp.concatenate([inner + start for start in outer], axis=0)
        dead[...] = jnp.where(position < lengths[slots[leaf]], 0.0, DEAD)
        attend(
            both[:, :HD], both[:, HD:],
            lambda block: jnp.concatenate([dead[block]] * (BR // HD), axis=1), False,
        )

    def attend_branch():
        wait_bytes(branch_landed.at[1], recv_p)

        def target(i):
            other = jnp.where(i >= 48, 1, 0)
            inner = i - 48 * other
            half = jnp.where(inner >= 24, 1, 0)
            return half * 48 + ((other + xl) & 1) * 24 + inner - 24 * half

        order = picks(target, 96, 96)
        for dy in range(8):
            y_from = (y - dy + 8) % 8
            rows = jnp.concatenate([branch_landed[0, dy], branch_landed[1, dy]], axis=0)
            ordered = moved(order, rows)
            branch_kv[0, y_from] = ordered[:48]
            branch_kv[1, y_from] = ordered[48:]
        attend(
            branch_kv[0].reshape(BR, HD), branch_kv[1].reshape(BR, HD),
            lambda block: shown[block], True,
        )

    def turn_queries():
        loads[5].wait()
        for head in range(HEADS):
            flipped = jnp.transpose(queries[:, head * HD : head * HD + HD])
            scaled = flipped.astype(jnp.float32) * SCORE_SCALE
            coarse = scaled.astype(jnp.bfloat16)
            fine = (scaled - coarse.astype(jnp.float32)).astype(jnp.bfloat16)
            columns = slice((head % 2) * BR, (head % 2) * BR + BR)
            turned[head // 2, :HD, columns] = coarse
            turned[head // 2, HD:, columns] = fine

    def mark_ancestors():
        loads[4].wait()
        above = lax.broadcasted_iota(jnp.int32, (HD, HD), 0)
        along = lax.broadcasted_iota(jnp.int32, (HD, HD), 1)

        def links(up, down):
            return above + up * HD == parents[:, down * HD : down * HD + HD]

        def as_picks(wanted):
            return jnp.where(wanted, 1.0, 0.0).astype(jnp.bfloat16)

        within = [as_picks(jnp.logical_or(links(b, b), above == along)) for b in range(3)]
        for _ in range(7):
            within = [
                as_picks(jnp.dot(one, one, preferred_element_type=jnp.float32) > 0.5)
                for one in within
            ]
        step_one = moved(as_picks(links(0, 1)), within[1])
        step_two = moved(as_picks(links(1, 2)), within[2])
        zero_one = moved(within[0], step_one)
        blocks = {
            (0, 0): within[0], (1, 1): within[1], (2, 2): within[2],
            (0, 1): zero_one, (1, 2): moved(within[1], step_two), (0, 2): moved(zero_one, step_two),
        }
        for up in range(3):
            for down in range(3):
                if (up, down) in blocks:
                    mask = jnp.where(blocks[up, down].astype(jnp.float32) > 0.5, 0.0, DEAD)
                else:
                    mask = jnp.full((HD, HD), DEAD, jnp.float32)
                shown[up * HD : up * HD + HD, down * HD : down * HD + HD] = mask

    def hand_branch():
        wait_bytes(branch_landed.at[0, 1:8], recv_r)
        pltpu.make_async_remote_copy(
            src_ref=branch_landed.at[0],
            dst_ref=branch_landed.at[1],
            send_sem=send_p,
            recv_sem=recv_p,
            device_id=near(0, 1, 0),
            device_id_type=MESH,
        ).start()

    send_plane(16, 48)
    pass_on(0)
    send_plane(48, 64)
    landed[63] = staged[0, y]
    turn_queries()
    pass_on(1)
    hand_branch()
    mark_ancestors()
    pass_on(2)
    pass_on(3)
    attend_branch()
    attend_chunk(0)
    attend_chunk(1)
    attend_chunk(2)
    attend_chunk(3)

    stores = []
    for head in range(HEADS):
        columns = slice((head % 2) * BR, (head % 2) * BR + BR)
        lanes = slice(head * HD, head * HD + HD)
        normal = summed[head // 2, :, columns] * (1.0 / total[head // 2, :, columns])
        result[:, lanes] = jnp.transpose(normal.astype(jnp.bfloat16))
        stores.append(pltpu.make_async_copy(result.at[:, lanes], out.at[:, lanes], store.at[head]))
        stores[-1].start()
    for one in stores:
        one.wait()

    wait_bytes(landed.at[0:63], send_a)
    wait_bytes(branch_landed.at[0, 1:8], send_r)
    wait_bytes(branch_landed.at[0], send_p)
    wait_bytes(keys_values.at[:, 1:8], send_b)


def local(trunk_kv, slot_trees, trunk_len, parents, queries, branch_kv):
    hbm = pl.BlockSpec(memory_space=pltpu.HBM)
    bf16, f32 = jnp.bfloat16, jnp.float32
    attended = pl.pallas_call(
        kernel,
        out_shape=jax.ShapeDtypeStruct((BR, HEADS * HD), bf16),
        in_specs=[hbm] * 6,
        out_specs=hbm,
        scratch_shapes=[
            pltpu.SMEM((TREES,), jnp.int32),
            pltpu.SMEM((TREES,), jnp.int32),
            pltpu.VMEM((TREES, 32, 256), bf16),
            pltpu.VMEM((192, 256), bf16),
            pltpu.VMEM((BR, HEADS * HD), bf16),
            pltpu.VMEM((1, BR), jnp.int32),
            pltpu.VMEM((128, 128), bf16),
            pltpu.VMEM((256, 256), bf16),
            pltpu.VMEM((8, 8, 16, 256), bf16),
            pltpu.VMEM((64, 16, 256), bf16),
            pltpu.VMEM((CHUNKS, 4, 64, 256), bf16),
            pltpu.VMEM((CHUNKS, 8, 64, 256), bf16),
            pltpu.VMEM((8, 48, HD), bf16),
            pltpu.VMEM((2, 8, 48, HD), bf16),
            pltpu.VMEM((2, 8, 48, HD), bf16),
            pltpu.VMEM((PAIRS, 2 * HD, WIDE), bf16),
            pltpu.VMEM((BR, BR), f32),
            pltpu.VMEM((PAIRS, 1, WIDE), f32),
            pltpu.VMEM((PAIRS, 1, WIDE), f32),
            pltpu.VMEM((PAIRS, HD, WIDE), f32),
            pltpu.VMEM((512, HD), f32),
            pltpu.VMEM((PAIRS, 512, WIDE), f32),
            pltpu.VMEM((PAIRS, 512, WIDE), bf16),
            pltpu.VMEM((BR, HEADS * HD), bf16),
            pltpu.SemaphoreType.DMA((6,)),
            pltpu.SemaphoreType.DMA,
            pltpu.SemaphoreType.DMA((CHUNKS,)),
            pltpu.SemaphoreType.DMA,
            pltpu.SemaphoreType.DMA((CHUNKS,)),
            pltpu.SemaphoreType.DMA,
            pltpu.SemaphoreType.DMA,
            pltpu.SemaphoreType.DMA,
            pltpu.SemaphoreType.DMA,
            pltpu.SemaphoreType.DMA((HEADS,)),
            pltpu.SemaphoreType.REGULAR,
        ],
        compiler_params=pltpu.CompilerParams(
            collective_id=0, has_side_effects=True, vmem_limit_bytes=60 * 1024 * 1024
        ),
    )(
        slot_trees,
        trunk_len,
        trunk_kv.reshape(TREES, 32, 2 * HD),
        branch_kv.reshape(192, 2 * HD),
        queries.reshape(BR, HEADS * HD),
        parents,
    )
    return attended.reshape(1, BR, HEADS * HD)


def solution(mesh):
    in_specs = (
        P(None, ("leaf", "tensor"), None, None),
        P(),
        P(),
        P("leaf", None),
        P("leaf", None, "tensor"),
        P("leaf", "tensor", None, None),
    )
    out_specs = P("leaf", None, "tensor")
    return jax.shard_map(local, mesh=mesh, in_specs=in_specs, out_specs=out_specs, check_vma=False)
```

```python
import math

import jax
import jax.numpy as jnp
from jax import lax
from jax.experimental import pallas as pl
from jax.experimental.pallas import tpu as pltpu
from jax.sharding import PartitionSpec as P

MESH = pl.DeviceIdType.MESH

HD = 128
BR = 384
TREES = 32
HEADS = 4
PAIRS = 2
WIDE = 2 * BR
CHUNKS = 4
BLOCK = 64
DEAD = -1e30
SCORE_SCALE = math.log2(math.e) / math.sqrt(HD)


def by_distance():
    def steps(pair):
        return min(pair[0], 8 - pair[0]) + min(pair[1], 8 - pair[1])

    ways = (4, 3, 5, 2, 6, 1, 7)
    first = [(0, dy) for dy in ways] + [(dz, 0) for dz in ways]
    others = sorted(((dz, dy) for dz in ways for dy in ways), key=lambda pair: -steps(pair))
    return first + others + [(0, 0)]


PLANE = by_distance()


def picks(target, rows, columns):
    row = lax.broadcasted_iota(jnp.int32, (rows, columns), 0)
    column = lax.broadcasted_iota(jnp.int32, (rows, columns), 1)
    return jnp.where(row == target(column), 1.0, 0.0).astype(jnp.bfloat16)


def moved(order, rows):
    return jnp.dot(order, rows, preferred_element_type=jnp.float32).astype(jnp.bfloat16)


def kernel(
    slots_hbm, lengths_hbm, trunk_hbm, branch_hbm, queries_hbm, parents_hbm,
    out,
    slots, lengths, trunk, branch, queries, parents, pick_head, pick_target,
    staged, landed, sorted_rows, keys_values, branch_staged, branch_landed, branch_kv,
    turned, shown, top, total, summed, dead, raw, rounded, result,
    load, send_a, recv_a, send_b, recv_b, send_r, recv_r, send_p, recv_p, store, rows_in,
):
    leaf = lax.axis_index("leaf")
    tensor = lax.axis_index("tensor")
    xh, z, c = leaf // 16, (leaf // 2) % 8, leaf % 2
    y, xl = tensor // 2, tensor % 2

    def place(xh, z, c, y, xl):
        return ((xh * 8 + z) * 2 + c, y * 2 + xl)

    def near(a, d, b):
        return place((xh + a) % 2, z, (c + b) % 2, y, (xl + d) % 2)

    barrier = pltpu.get_barrier_semaphore()
    ring = ((1, 0, 0), (1, 0, 1), (1, 1, 0), (1, 1, 1), (0, 1, 0), (0, 1, 1), (0, 0, 1))

    def signal(where):
        pl.semaphore_signal(barrier, inc=1, device_id=where, device_id_type=MESH)

    for step in range(1, 8):
        signal(place(xh, z, c, (y + step) % 8, xl))
        signal(place(xh, (z + step) % 8, c, y, xl))
    for flips in ring:
        signal(near(*flips))

    loads = [
        pltpu.make_async_copy(there, here, load.at[which])
        for which, (there, here) in enumerate(
            [
                (slots_hbm, slots), (trunk_hbm, trunk), (lengths_hbm, lengths),
                (branch_hbm, branch), (parents_hbm, parents), (queries_hbm, queries),
            ]
        )
    ]
    for one in loads:
        one.start()
    pick_head[...] = picks(
        lambda i: (i & 7) * 16 + (i >> 5) * 4 + ((i >> 3) & 3), 128, 128
    )
    pick_target[...] = picks(
        lambda i: ((i >> 2) & 3) * 64 + (i >> 4) * 4 + (i & 3), 256, 256
    )

    def stage(dz):
        z_to = (z + dz) % 8
        rows = jnp.concatenate(
            [trunk[slots[((q // 2) * 8 + z_to) * 2 + q % 2]] for q in range(4)], axis=0
        )
        ordered = moved(pick_head[...], rows)
        for head in range(8):
            staged[dz, head] = ordered[head * 16 : head * 16 + 16]

    def send_plane(first, end):
        for at in range(first, end):
            dz, dy = PLANE[at]
            if dz or dy:
                y_to = (y + dy) % 8
                pltpu.make_async_remote_copy(
                    src_ref=staged.at[dz, y_to],
                    dst_ref=landed.at[at],
                    send_sem=send_a,
                    recv_sem=recv_a.at[at // 16],
                    device_id=place(xh, (z + dz) % 8, c, y_to, xl),
                    device_id_type=MESH,
                ).start()

    loads[0].wait()
    loads[1].wait()
    stage(0)
    pl.semaphore_wait(barrier, 14 + len(ring))
    for step in range(1, 8):
        pl.semaphore_signal(
            rows_in, inc=1, device_id=place(xh, (z + step) % 8, c, y, xl), device_id_type=MESH
        )
    send_plane(0, 7)
    for at in range(7, 14):
        stage(PLANE[at][0])
        send_plane(at, at + 1)
    pl.semaphore_wait(rows_in, 7)
    send_plane(14, 16)

    loads[3].wait()

    def branch_target(i):
        half = jnp.where(i >= 192, 1, 0)
        inner = i - 192 * half
        return (inner & 7) * 48 + half * 24 + (inner >> 3)

    rows = jnp.concatenate([branch[:, :HD], branch[:, HD:]], axis=0)
    ordered = moved(picks(branch_target, 384, 384), rows)
    for head in range(8):
        branch_staged[head] = ordered[head * 48 : head * 48 + 48]
    for dy in (4, 3, 5, 2, 6, 1, 7):
        y_to = (y + dy) % 8
        pltpu.make_async_remote_copy(
            src_ref=branch_staged.at[y_to],
            dst_ref=branch_landed.at[0, dy],
            send_sem=send_r,
            recv_sem=recv_r,
            device_id=place(xh, z, c, y_to, xl),
            device_id_type=MESH,
        ).start()
    branch_landed[0, 0] = branch_staged[y]

    def wait_bytes(ref, sem):
        pltpu.make_async_copy(ref, ref, sem).wait()

    def pass_on(chunk):
        first = chunk * 16
        wait_bytes(landed.at[first : first + (15 if chunk == 3 else 16)], recv_a.at[chunk])
        rows = landed[first : first + 16].reshape(256, 256)
        ordered = moved(pick_target[...], rows)
        for target in range(4):
            sorted_rows[chunk, target] = ordered[target * 64 : target * 64 + 64]
        for a, d, b in ring:
            target = ((xh + a) % 2) * 2 + (c + b) % 2
            pltpu.make_async_remote_copy(
                src_ref=sorted_rows.at[chunk, target],
                dst_ref=keys_values.at[chunk, a * 4 + d * 2 + b],
                send_sem=send_b,
                recv_sem=recv_b.at[chunk],
                device_id=near(a, d, b),
                device_id_type=MESH,
            ).start()
        keys_values[chunk, 0] = sorted_rows[chunk, xh * 2 + c]

    def attend(keys, values, mask_rows, first):
        count = keys.shape[0]
        keys = jnp.concatenate([keys, keys], axis=1)
        values = jnp.transpose(values)
        blocks = [slice(at, at + BLOCK) for at in range(0, count, BLOCK)]
        for pair in range(PAIRS):
            raw[pair, :count] = jnp.dot(keys, turned[pair], preferred_element_type=jnp.float32)
        for pair in range(PAIRS):
            fades = []
            for half in range(2):
                columns = slice(half * BR, half * BR + BR)
                best = None if first else top[pair, :, columns]
                for block in blocks:
                    scores = raw[pair, block, columns] + mask_rows(block)
                    highest = jnp.max(scores, axis=0, keepdims=True)
                    best = highest if best is None else jnp.maximum(best, highest)
                weight_sum = None
                for block in blocks:
                    weights = jnp.exp2(raw[pair, block, columns] + mask_rows(block) - best)
                    part = jnp.sum(weights, axis=0, keepdims=True)
                    weight_sum = part if weight_sum is None else weight_sum + part
                    rounded[pair, block, columns] = weights.astype(jnp.bfloat16)
                if not first:
                    fades.append(jnp.exp2(top[pair, :, columns] - best))
                    weight_sum = total[pair, :, columns] * fades[half] + weight_sum
                total[pair, :, columns] = weight_sum
                top[pair, :, columns] = best
            product = jnp.dot(
                values, rounded[pair, :count], preferred_element_type=jnp.float32
            )
            for half in range(2):
                columns = slice(half * BR, half * BR + BR)
                if first:
                    summed[pair, :, columns] = product[:, columns]
                else:
                    summed[pair, :, columns] = (
                        summed[pair, :, columns] * fades[half] + product[:, columns]
                    )

    def attend_chunk(chunk):
        if chunk == 0:
            loads[2].wait()
        wait_bytes(keys_values.at[chunk, 1:8], recv_b.at[chunk])
        both = keys_values[chunk].reshape(512, 256)
        row = lax.broadcasted_iota(jnp.int32, (64, HD), 0)
        inner = row & 3
        for at in range(16):
            dz, dy = PLANE[chunk * 16 + at]
            start = ((z - dz + 8) % 8) * 128 + ((y - dy + 8) % 8) * 8
            inner = inner + jnp.where((row >> 2) == at, start, 0)
        outer = [
            (((xh + a) % 2) * 16 + (c + b) % 2) * 64 + ((xl + d) % 2) * 4
            for a in range(2) for d in range(2) for b in range(2)
        ]
        position = jnp.concatenate([inner + start for start in outer], axis=0)
        dead[...] = jnp.where(position < lengths[slots[leaf]], 0.0, DEAD)
        attend(
            both[:, :HD], both[:, HD:],
            lambda block: jnp.concatenate([dead[block]] * (BR // HD), axis=1), False,
        )

    def attend_branch():
        wait_bytes(branch_landed.at[1], recv_p)

        def target(i):
            other = jnp.where(i >= 48, 1, 0)
            inner = i - 48 * other
            half = jnp.where(inner >= 24, 1, 0)
            return half * 48 + ((other + xl) & 1) * 24 + inner - 24 * half

        order = picks(target, 96, 96)
        for dy in range(8):
            y_from = (y - dy + 8) % 8
            rows = jnp.concatenate([branch_landed[0, dy], branch_landed[1, dy]], axis=0)
            ordered = moved(order, rows)
            branch_kv[0, y_from] = ordered[:48]
            branch_kv[1, y_from] = ordered[48:]
        attend(
            branch_kv[0].reshape(BR, HD), branch_kv[1].reshape(BR, HD),
            lambda block: shown[block], True,
        )

    def turn_queries():
        loads[5].wait()
        for head in range(HEADS):
            flipped = jnp.transpose(queries[:, head * HD : head * HD + HD])
            scaled = flipped.astype(jnp.float32) * SCORE_SCALE
            coarse = scaled.astype(jnp.bfloat16)
            fine = (scaled - coarse.astype(jnp.float32)).astype(jnp.bfloat16)
            columns = slice((head % 2) * BR, (head % 2) * BR + BR)
            turned[head // 2, :HD, columns] = coarse
            turned[head // 2, HD:, columns] = fine

    def mark_ancestors():
        loads[4].wait()
        above = lax.broadcasted_iota(jnp.int32, (HD, HD), 0)
        along = lax.broadcasted_iota(jnp.int32, (HD, HD), 1)

        def links(up, down):
            return above + up * HD == parents[:, down * HD : down * HD + HD]

        def as_picks(wanted):
            return jnp.where(wanted, 1.0, 0.0).astype(jnp.bfloat16)

        within = [as_picks(jnp.logical_or(links(b, b), above == along)) for b in range(3)]
        for _ in range(7):
            within = [
                as_picks(jnp.dot(one, one, preferred_element_type=jnp.float32) > 0.5)
                for one in within
            ]
        step_one = moved(as_picks(links(0, 1)), within[1])
        step_two = moved(as_picks(links(1, 2)), within[2])
        zero_one = moved(within[0], step_one)
        blocks = {
            (0, 0): within[0], (1, 1): within[1], (2, 2): within[2],
            (0, 1): zero_one, (1, 2): moved(within[1], step_two), (0, 2): moved(zero_one, step_two),
        }
        for up in range(3):
            for down in range(3):
                if (up, down) in blocks:
                    mask = jnp.where(blocks[up, down].astype(jnp.float32) > 0.5, 0.0, DEAD)
                else:
                    mask = jnp.full((HD, HD), DEAD, jnp.float32)
                shown[up * HD : up * HD + HD, down * HD : down * HD + HD] = mask

    def hand_branch():
        wait_bytes(branch_landed.at[0, 1:8], recv_r)
        pltpu.make_async_remote_copy(
            src_ref=branch_landed.at[0],
            dst_ref=branch_landed.at[1],
            send_sem=send_p,
            recv_sem=recv_p,
            device_id=near(0, 1, 0),
            device_id_type=MESH,
        ).start()

    send_plane(16, 48)
    pass_on(0)
    send_plane(48, 64)
    landed[63] = staged[0, y]
    turn_queries()
    pass_on(1)
    hand_branch()
    pass_on(2)
    pass_on(3)
    mark_ancestors()
    attend_branch()
    attend_chunk(0)
    attend_chunk(1)
    attend_chunk(2)
    attend_chunk(3)

    stores = []
    for head in range(HEADS):
        columns = slice((head % 2) * BR, (head % 2) * BR + BR)
        lanes = slice(head * HD, head * HD + HD)
        normal = summed[head // 2, :, columns] * (1.0 / total[head // 2, :, columns])
        result[:, lanes] = jnp.transpose(normal.astype(jnp.bfloat16))
        stores.append(pltpu.make_async_copy(result.at[:, lanes], out.at[:, lanes], store.at[head]))
        stores[-1].start()
    for one in stores:
        one.wait()

    wait_bytes(landed.at[0:63], send_a)
    wait_bytes(branch_landed.at[0, 1:8], send_r)
    wait_bytes(branch_landed.at[0], send_p)
    wait_bytes(keys_values.at[:, 1:8], send_b)


def local(trunk_kv, slot_trees, trunk_len, parents, queries, branch_kv):
    hbm = pl.BlockSpec(memory_space=pltpu.HBM)
    bf16, f32 = jnp.bfloat16, jnp.float32
    attended = pl.pallas_call(
        kernel,
        out_shape=jax.ShapeDtypeStruct((BR, HEADS * HD), bf16),
        in_specs=[hbm] * 6,
        out_specs=hbm,
        scratch_shapes=[
            pltpu.SMEM((TREES,), jnp.int32),
            pltpu.SMEM((TREES,), jnp.int32),
            pltpu.VMEM((TREES, 32, 256), bf16),
            pltpu.VMEM((192, 256), bf16),
            pltpu.VMEM((BR, HEADS * HD), bf16),
            pltpu.VMEM((1, BR), jnp.int32),
            pltpu.VMEM((128, 128), bf16),
            pltpu.VMEM((256, 256), bf16),
            pltpu.VMEM((8, 8, 16, 256), bf16),
            pltpu.VMEM((64, 16, 256), bf16),
            pltpu.VMEM((CHUNKS, 4, 64, 256), bf16),
            pltpu.VMEM((CHUNKS, 8, 64, 256), bf16),
            pltpu.VMEM((8, 48, HD), bf16),
            pltpu.VMEM((2, 8, 48, HD), bf16),
            pltpu.VMEM((2, 8, 48, HD), bf16),
            pltpu.VMEM((PAIRS, 2 * HD, WIDE), bf16),
            pltpu.VMEM((BR, BR), f32),
            pltpu.VMEM((PAIRS, 1, WIDE), f32),
            pltpu.VMEM((PAIRS, 1, WIDE), f32),
            pltpu.VMEM((PAIRS, HD, WIDE), f32),
            pltpu.VMEM((512, HD), f32),
            pltpu.VMEM((PAIRS, 512, WIDE), f32),
            pltpu.VMEM((PAIRS, 512, WIDE), bf16),
            pltpu.VMEM((BR, HEADS * HD), bf16),
            pltpu.SemaphoreType.DMA((6,)),
            pltpu.SemaphoreType.DMA,
            pltpu.SemaphoreType.DMA((CHUNKS,)),
            pltpu.SemaphoreType.DMA,
            pltpu.SemaphoreType.DMA((CHUNKS,)),
            pltpu.SemaphoreType.DMA,
            pltpu.SemaphoreType.DMA,
            pltpu.SemaphoreType.DMA,
            pltpu.SemaphoreType.DMA,
            pltpu.SemaphoreType.DMA((HEADS,)),
            pltpu.SemaphoreType.REGULAR,
        ],
        compiler_params=pltpu.CompilerParams(
            collective_id=0, has_side_effects=True, vmem_limit_bytes=60 * 1024 * 1024
        ),
    )(
        slot_trees,
        trunk_len,
        trunk_kv.reshape(TREES, 32, 2 * HD),
        branch_kv.reshape(192, 2 * HD),
        queries.reshape(BR, HEADS * HD),
        parents,
    )
    return attended.reshape(1, BR, HEADS * HD)


def solution(mesh):
    in_specs = (
        P(None, ("leaf", "tensor"), None, None),
        P(),
        P(),
        P("leaf", None),
        P("leaf", None, "tensor"),
        P("leaf", "tensor", None, None),
    )
    out_specs = P("leaf", None, "tensor")
    return jax.shard_map(local, mesh=mesh, in_specs=in_specs, out_specs=out_specs, check_vma=False)
```
